32 devices in a mesh: groups: 2 (over y), tm: 4 (over z), rows: 4 (over x, core).
Axes of the slice: x: 2, y: 2, z: 4, core: 2. Of those that a mesh axis runs over, the one named last changes fastest.
Arguments:
- latents: bfloat16 [16, 16, 128, 256], P(('groups', 'tm'), 'rows'), parts along dimension 0, may hold values from -6 to 6
- weight_in: bfloat16 [3, 3, 256, 256], replicated, may hold values from -0.125 to 0.125
- weight_out: bfloat16 [3, 3, 256, 256], replicated, may hold values from -0.0234375 to 0.0234375
- decay_table: float32 [16], replicated, may hold values from 0.99 to 0.999
- decay_index: int32 [256], replicated, may hold values from 0 to 15
Outputs:
- updated: bfloat16 [16, 16, 128, 256], P(('groups', 'tm'), 'rows'), parts along dimension 0
The draws below stay inside these ranges and needn't reach their ends.
There are 2 independent parts, one for each index of `groups`. The reference program is written for one: setup_inputs(seed, part) draws one part's arguments, and reference() takes and returns one part's arrays. A program takes and returns all parts, laid end to end along the dimension named above; an argument that names none is the same for every part. Nothing has to cross between parts.
All inputs are finite; a program needn't handle non-finite values.
Results may differ from the reference program's by a relative error of at most 0.0032.
Values may be sent and summed in bfloat16 or wider, within the bound.
No kernel may reach another device: no remote copies, remote signals or barrier semaphores. Data moves between devices by JAX's collectives and lax.ppermute only.
A program may use at most 64 MiB of HBM per device.

```python
import jax
import jax.numpy as jnp
from jax import lax

C = 256
W = 128
LEVELS = 16
FRAMES = 8
H = 16


def place_ends(drawn, stream_key, smallest, largest):
    longest = drawn.shape.index(max(drawn.shape))
    spots = []
    for shift in (0, 1):
        where = [jax.random.randint(jax.random.fold_in(stream_key, axis), (), 0, length) for axis, length in enumerate(drawn.shape)]
        where[longest] = (where[longest] + shift) % drawn.shape[longest]
        spots.append(tuple(where))
    return drawn.at[spots[0]].set(smallest).at[spots[1]].set(largest)


def block_levels(key, extent, pieces, low, largest):
    gain = 1.0
    for position, shards_of in pieces:
        draws = jax.random.uniform(jax.random.fold_in(jax.random.fold_in(key, 6), position), (shards_of,), jnp.float32, low / len(pieces), largest / len(pieces))
        gain = gain * jnp.repeat(jnp.exp(draws), extent[position] // shards_of).reshape((-1,) + (1,) * (len(extent) - 1 - position))
    return gain


def centred(stream_key, shape, scale, most, shards=(), dtype=jnp.bfloat16):
    gain = block_levels(stream_key, shape, shards, -0.22, 0.18) if shards else 1.0
    drawn = jax.random.normal(stream_key, shape, jnp.float32) * scale * gain
    return jnp.minimum(jnp.maximum(drawn, -most), most).astype(dtype)


def setup_inputs(seed: int = 0, part: int = 0) -> dict:
    key_list = jax.random.split(jax.random.key(seed), 6)
    part_keys = jax.random.split(jax.random.fold_in(key_list[5], part), 6)
    return {
        "latents": centred(part_keys[0], (FRAMES, H, W, C), 1.0, 6.0, ((0, 4), (1, 4))),
        "weight_in": centred(key_list[1], (3, 3, C, C), (9 * C) ** -0.5, 0.125),
        "weight_out": centred(key_list[2], (3, 3, C, C), (9 * C * 32) ** -0.5, 0.0234375),
        "decay_table": jnp.clip(jax.random.uniform(key_list[3], (LEVELS,), jnp.float32, 0.99, 0.999), 0.99, 0.999),
        "decay_index": place_ends(jax.random.randint(key_list[4], (C,), 0, LEVELS), jax.random.fold_in(key_list[4], 1), 0, LEVELS - 1).astype(jnp.int32),
    }


def convolve(source, weight):
    padded = jnp.pad(source, ((0, 0), (1, 1), (1, 1), (0, 0)))
    height = source.shape[1]
    width = source.shape[2]
    depth = weight.shape[2]

    def one_frame(image):
        total = jnp.zeros((height * width, weight.shape[3]), jnp.float32)
        for tap_row in range(3):
            for tap_col in range(3):
                window = image[tap_row:tap_row + height, tap_col:tap_col + width, :].reshape(-1, depth)
                total = total + jnp.dot(window, weight[tap_row, tap_col], preferred_element_type=jnp.float32)
        return total.reshape(height, width, weight.shape[3])

    return lax.map(one_frame, padded)


def reference(latents, weight_in, weight_out, decay_table, decay_index):
    decays = decay_table[decay_index.astype(jnp.int32)]
    driven = convolve(latents, weight_in)

    def advance(running, incoming):
        running = decays * running + incoming
        return running, running

    start = jnp.zeros(latents.shape[1:], jnp.float32)
    _, states = lax.scan(advance, start, driven)
    rounded = states.astype(jnp.bfloat16)
    mixed = convolve(rounded, weight_out)
    return (latents.astype(jnp.float32) + jax.nn.gelu(mixed)).astype(jnp.bfloat16)
```

```python
import functools

import jax
import jax.numpy as jnp
from jax import lax
from jax.experimental import pallas as pl
from jax.experimental.pallas import tpu as pltpu
from jax.sharding import PartitionSpec as P

VMEM = pl.BlockSpec(memory_space=pltpu.VMEM)
ANY = pl.BlockSpec(memory_space=pl.ANY)
LIMIT = 24 * 1024 * 1024


def matmul(rows, weight):
    lead, depth = rows.shape[:-1], rows.shape[-1]
    flat = jnp.dot(rows.reshape(-1, depth), weight, preferred_element_type=jnp.float32)
    return flat.reshape(*lead, weight.shape[-1])


def join_columns(left, middle, right):
    width = middle.shape[-2]
    axis = middle.ndim - 2
    column = lax.broadcasted_iota(jnp.int32, middle.shape, axis)
    left = jnp.where(column == 0, 0.0, pltpu.roll(left, 1, axis))
    right = jnp.where(column == width - 1, 0.0, pltpu.roll(right, width - 1, axis))
    return left + middle + right


def own_rows(x_ref, w_ref, taps):
    frames, strip = x_ref.shape[:2]
    for q in range(3):
        for f in range(frames):
            taps[q, f] = matmul(x_ref[f], w_ref[1, q])
            taps[q, f, 1:] += matmul(x_ref[f, : strip - 1], w_ref[0, q])
            taps[q, f, : strip - 1] += matmul(x_ref[f, 1:], w_ref[2, q])


def edge_rows(low_ref, high_ref, w_ref, axis):
    mine, count = lax.axis_index(axis), lax.axis_size(axis)
    low, high = low_ref[...], high_ref[...]
    low = jnp.where(mine > 0, low, jnp.zeros_like(low))
    high = jnp.where(mine < count - 1, high, jnp.zeros_like(high))
    first = join_columns(*[matmul(low, w_ref[0, q]) for q in range(3)])
    last = join_columns(*[matmul(high, w_ref[2, q]) for q in range(3)])
    return first, last


def drive_kernel(x_ref, w_ref, decay_ref, inner_ref, outer_ref, sent_ref, taps):
    frames, strip = x_ref.shape[:2]
    own_rows(x_ref, w_ref, taps)
    decay = decay_ref[...].reshape(1, 1, -1)
    state = None
    for f in range(frames):
        driven = join_columns(taps[0, f], taps[1, f], taps[2, f])
        state = driven if state is None else decay * state + driven
        inner_ref[f] = state[1 : strip - 1]
        outer_ref[f, 0] = state[0]
        outer_ref[f, 1] = state[strip - 1]
    sent_ref[...] = state[1 : strip - 1].astype(sent_ref.dtype)


def drive_edge_kernel(low_ref, high_ref, w_ref, decay_ref, outer_ref, result_ref, sent_ref):
    frames = outer_ref.shape[0]
    first, last = edge_rows(low_ref, high_ref, w_ref, "rows")
    decay = decay_ref[...]
    for side, driven in ((0, first), (1, last)):
        more = None
        for f in range(frames):
            now = driven[f, 0]
            more = now if more is None else decay * more + now
            state = outer_ref[f, side] + more
            result_ref[f, side] = state
        sent_ref[side] = state.astype(sent_ref.dtype)


def residual(x, mixed):
    return (x.astype(jnp.float32) + jax.nn.gelu(mixed)).astype(jnp.bfloat16)


def mix_kernel(inner_ref, carried_ref, growth_ref, outer_ref, w_ref, x_ref, out_ref, edge_ref, states, taps, ready, sem):
    frames, strip = states.shape[:2]
    carried = carried_ref[...]
    for f in range(frames):
        growth = growth_ref[f].reshape(1, 1, -1)
        states[f, 1 : strip - 1] = (inner_ref[f] + growth * carried).astype(jnp.bfloat16)
        states[f, 0] = outer_ref[f, 0]
        states[f, strip - 1] = outer_ref[f, 1]
    own_rows(states, w_ref, taps)
    for f in range(frames):
        mixed = join_columns(taps[0, f], taps[1, f], taps[2, f])
        ready[f] = residual(x_ref[f, 1 : strip - 1], mixed[1 : strip - 1])
        edge_ref[f, 0] = mixed[0]
        edge_ref[f, 1] = mixed[strip - 1]
    copy = pltpu.make_async_copy(ready, out_ref.at[:, 1 : strip - 1], sem)
    copy.start()
    copy.wait()


def mix_edge_kernel(low_ref, high_ref, w_ref, edge_ref, x_ref, before_ref, out_ref, ready, sems):
    frames, strip = x_ref.shape[:2]
    first, last = edge_rows(low_ref, high_ref, w_ref, "rows")
    copies = []
    for side, row, more in ((0, 0, first), (1, strip - 1, last)):
        ready[side] = residual(x_ref[:, row], edge_ref[:, side] + more[:, 0])
        copy = pltpu.make_async_copy(ready.at[side], out_ref.at[:, row], sems.at[side])
        copy.start()
        copies.append(copy)
    for copy in copies:
        copy.wait()


def kernel_call(kernel, out_shape, in_specs, out_specs, scratch, flops, aliases=None):
    return pl.pallas_call(
        kernel,
        out_shape=out_shape,
        in_specs=in_specs,
        out_specs=out_specs,
        scratch_shapes=scratch,
        input_output_aliases=aliases or {},
        compiler_params=pltpu.CompilerParams(vmem_limit_bytes=LIMIT),
        cost_estimate=pl.CostEstimate(flops=flops, bytes_accessed=1 << 20, transcendentals=0),
    )


def ring_halo(first, last, axis):
    count = lax.axis_size(axis)
    up = [(i, (i + 1) % count) for i in range(count)]
    down = [(target, source) for source, target in up]
    return lax.ppermute(last, axis, up), lax.ppermute(first, axis, down)


def swapped(value, axis, distance):
    return lax.ppermute(value, axis, [(i, i ^ distance) for i in range(lax.axis_size(axis))])


def butterfly(value, decay, axis):
    count, mine = lax.axis_size(axis), lax.axis_index(axis)
    total, carried, distance = value, None, 1
    before = jnp.ones_like(decay)
    while distance < count:
        other = swapped(total, axis, distance).astype(jnp.float32)
        after = (mine & distance) != 0
        own = total.astype(jnp.float32)
        here = jnp.where(after, before * other, 0.0)
        carried = here if carried is None else carried + here
        if 2 * distance < count:
            earlier, later = jnp.where(after, other, own), jnp.where(after, own, other)
            total = (decay * earlier + later).astype(value.dtype)
            before = jnp.where(after, decay * before, before)
            decay = decay * decay
        distance *= 2
    return carried


def far_first(value, decay, axis):
    mine = lax.axis_index(axis)
    far = swapped(value, axis, 2).astype(jnp.float32)
    far = jnp.where(mine >= 2, far, 0.0)
    message = jnp.where((mine & 1) != 0, far, decay * decay * far + value.astype(jnp.float32))
    near = swapped(message.astype(value.dtype), axis, 1).astype(jnp.float32)
    return jnp.where(mine >= 1, near, 0.0) + decay * far


def local(latents, weight_in, weight_out, decay_table, decay_index):
    frames, strip, width, channels = latents.shape
    levels = decay_table.shape[0]
    f32, bf16 = jnp.float32, jnp.bfloat16
    shaped = jax.ShapeDtypeStruct
    area = width * channels
    conv_flops = 2 * 9 * frames * strip * area * channels

    low, high = ring_halo(latents[:, :1], latents[:, strip - 1 :], "rows")
    onehot = decay_index[:, None] == jnp.arange(levels, dtype=jnp.int32)[None, :]
    decays = jnp.sum(jnp.where(onehot, decay_table[None, :], 0.0), axis=1)[None, :]
    growth = [decays]
    for _ in range(frames - 1):
        growth.append(growth[-1] * decays)
    over = growth[-1]
    growth = jnp.stack(growth)

    inner, outer, sent = kernel_call(
        drive_kernel,
        (shaped((frames, strip - 2, width, channels), f32), shaped((frames, 2, width, channels), f32), shaped((strip - 2, width, channels), bf16)),
        [VMEM] * 3,
        (VMEM,) * 3,
        [pltpu.VMEM((3, frames, strip, width, channels), f32)],
        conv_flops,
    )(latents, weight_in, decays)
    outer, edge_sent = kernel_call(
        drive_edge_kernel,
        (shaped((frames, 2, width, channels), f32), shaped((2, width, channels), bf16)),
        [VMEM] * 5,
        (VMEM,) * 2,
        [],
        conv_flops // 6,
        aliases={4: 0},
    )(low, high, weight_in, decays, outer)

    count = lax.axis_size("tm")
    scan = far_first if count == 4 else butterfly
    carried = scan(sent, over, "tm")
    edge_carried = butterfly(edge_sent, over, "tm")

    edge_states = (outer + growth[:, None] * edge_carried[None]).astype(bf16)
    low, high = ring_halo(edge_states[:, :1], edge_states[:, 1:], "rows")
    out, edge = kernel_call(
        mix_kernel,
        (shaped(latents.shape, bf16), shaped((frames, 2, width, channels), f32)),
        [VMEM] * 6,
        (ANY, VMEM),
        [
            pltpu.VMEM(latents.shape, bf16),
            pltpu.VMEM((3, frames, strip, width, channels), f32),
            pltpu.VMEM((frames, strip - 2, width, channels), bf16),
            pltpu.SemaphoreType.DMA,
        ],
        conv_flops,
    )(inner, carried, growth, edge_states, weight_out, latents)
    return kernel_call(
        mix_edge_kernel,
        shaped(latents.shape, bf16),
        [VMEM] * 5 + [ANY],
        ANY,
        [pltpu.VMEM((2, frames, width, channels), bf16), pltpu.SemaphoreType.DMA((2,))],
        conv_flops // 6,
        aliases={5: 0},
    )(low, high, weight_out, edge, latents, out)


def solution(mesh):
    in_specs = (P(("groups", "tm"), "rows", None, None), P(), P(), P(), P())
    out_specs = P(("groups", "tm"), "rows", None, None)
    return jax.shard_map(local, mesh=mesh, in_specs=in_specs, out_specs=out_specs, check_vma=False)
```

```python
import functools

import jax
import jax.numpy as jnp
from jax import lax
from jax.experimental import pallas as pl
from jax.experimental.pallas import tpu as pltpu
from jax.sharding import PartitionSpec as P

VMEM = pl.BlockSpec(memory_space=pltpu.VMEM)
ANY = pl.BlockSpec(memory_space=pl.ANY)
SMALL = 1000
LONG = 3000000000
LIMIT = 24 * 1024 * 1024
F32, BF16 = jnp.float32, jnp.bfloat16


def turned():
    return lax.axis_index("rows") % 2


def place(row, count):
    return jnp.where(turned() == 1, count - 1 - row, row)


def matmul(rows, weight):
    lead, depth = rows.shape[:-1], rows.shape[-1]
    flat = jnp.dot(rows.reshape(-1, depth), weight, preferred_element_type=F32)
    return flat.reshape(*lead, weight.shape[-1])


def join_columns(left, middle, right):
    width = middle.shape[-2]
    axis = middle.ndim - 2
    column = lax.broadcasted_iota(jnp.int32, middle.shape, axis)
    left = jnp.where(column == 0, 0.0, pltpu.roll(left, 1, axis))
    right = jnp.where(column == width - 1, 0.0, pltpu.roll(right, width - 1, axis))
    return left + middle + right


def own_rows(x_ref, w_ref, taps):
    frames, strip = x_ref.shape[:2]
    for q in range(3):
        for f in range(frames):
            taps[q, f] = matmul(x_ref[f], w_ref[1, q])
            taps[q, f, 1:] += matmul(x_ref[f, : strip - 1], w_ref[0, q])
            taps[q, f, : strip - 1] += matmul(x_ref[f, 1:], w_ref[2, q])


def from_outside(halo_ref, w_ref):
    mine, count = lax.axis_index("rows"), lax.axis_size("rows")
    halo = halo_ref[...]
    inside = jnp.logical_and(mine > 0, mine < count - 1)
    halo = jnp.where(inside, halo, jnp.zeros_like(halo))
    return join_columns(*[matmul(halo, w_ref[place(0, 3), q]) for q in range(3)])


def from_inside(halo_ref, w_ref):
    return join_columns(*[matmul(halo_ref[...], w_ref[place(2, 3), q]) for q in range(3)])


def rows_kernel(x_ref, outer_ref, inner_ref):
    frames, strip = x_ref.shape[:2]
    for f in range(frames):
        outer_ref[f] = x_ref[f, place(0, strip)]
        inner_ref[f] = x_ref[f, place(strip - 1, strip)]


def drive_kernel(x_ref, w_ref, table_ref, index_ref, outer_ref, middle_ref, inner_ref, sent_ref, growth_ref, taps, states):
    frames, strip = x_ref.shape[:2]
    own_rows(x_ref, w_ref, taps)
    index = index_ref[...]
    decay = jnp.zeros(index.shape, F32)
    for level in range(table_ref.shape[1]):
        decay = jnp.where(index == level, table_ref[:, level : level + 1], decay)
    growth = decay
    state = None
    for f in range(frames):
        growth_ref[f] = growth
        growth = growth * decay
        driven = join_columns(taps[0, f], taps[1, f], taps[2, f])
        state = driven if state is None else decay.reshape(1, 1, -1) * state + driven
        states[...] = state
        outer_ref[f] = states[place(0, strip)]
        middle_ref[f] = state[1 : strip - 1]
        inner_ref[f] = states[place(strip - 1, strip)]
    sent_ref[...] = state[1 : strip - 1].astype(BF16)


def drive_edge_kernel(beyond, halo_ref, w_ref, growth_ref, row_ref, result_ref, sent_ref, order_ref):
    frames = row_ref.shape[0]
    driven = beyond(halo_ref, w_ref)
    decay = growth_ref[0]
    more = None
    for f in range(frames):
        more = driven[f] if more is None else decay * more + driven[f]
        state = row_ref[f] + more
        result_ref[f] = state
    sent_ref[...] = state.astype(BF16)
    order_ref[...] = growth_ref[...]


def pair_kernel(own_ref, other_ref, growth_ref, total_ref, order_ref):
    over = growth_ref[growth_ref.shape[0] - 1]
    own, other = own_ref[...].astype(F32), other_ref[...].astype(F32)
    after = lax.axis_index("tm") % 2 == 1
    earlier, later = jnp.where(after, other, own), jnp.where(after, own, other)
    total_ref[...] = (over * earlier + later).astype(BF16)
    order_ref[...] = growth_ref[...]


def edge_states_kernel(row_ref, near_ref, far_ref, growth_ref, states_ref, order_ref):
    frames = row_ref.shape[0]
    over = growth_ref[frames - 1]
    mine = lax.axis_index("tm")
    near, far = near_ref[...].astype(F32), far_ref[...].astype(F32)
    far = jnp.where(mine >= 2, far, 0.0)
    carried = jnp.where(mine % 2 == 1, over * far + near, far)
    for f in range(frames):
        states_ref[f] = (row_ref[f] + growth_ref[f] * carried).astype(BF16)
    order_ref[...] = growth_ref[...]


def relay_kernel(own_ref, before_ref, growth_ref, message_ref, order_ref):
    over = growth_ref[growth_ref.shape[0] - 1]
    message_ref[...] = (over * before_ref[...].astype(F32) + own_ref[...].astype(F32)).astype(BF16)
    order_ref[...] = growth_ref[...]


def middle_states_kernel(middle_ref, first_ref, second_ref, third_ref, growth_ref, states_ref):
    frames = middle_ref.shape[0]
    mine = lax.axis_index("tm")
    carried = jnp.zeros(first_ref.shape, F32)
    for hop, ref in enumerate((first_ref, second_ref, third_ref)):
        carried = jnp.where(mine == hop + 1, ref[...].astype(F32), carried)
    for f in range(frames):
        states_ref[f] = (middle_ref[f] + growth_ref[f] * carried).astype(BF16)


def residual(x, mixed):
    return (x.astype(F32) + jax.nn.gelu(mixed)).astype(BF16)


def mix_kernel(outer_in, middle_in, inner_in, w_ref, x_ref, outer_ref, middle_ref, inner_ref, states, taps):
    frames, strip = x_ref.shape[:2]
    for f in range(frames):
        states[f, place(0, strip)] = outer_in[f]
        states[f, 1 : strip - 1] = middle_in[f]
        states[f, place(strip - 1, strip)] = inner_in[f]
    own_rows(states, w_ref, taps)
    for f in range(frames):
        mixed = join_columns(taps[0, f], taps[1, f], taps[2, f])
        middle_ref[f] = residual(x_ref[f, 1 : strip - 1], mixed[1 : strip - 1])
        first, last = mixed[0], mixed[strip - 1]
        outer_ref[f] = jnp.where(turned() == 1, last, first)
        inner_ref[f] = jnp.where(turned() == 1, first, last)


def finish_kernel(outer_halo, inner_halo, w_ref, outer_ref, inner_ref, middle_ref, x_ref, out_ref, ready, sems):
    frames, strip = x_ref.shape[:2]
    copies = []

    def send(source, target):
        copies.append(pltpu.make_async_copy(source, target, sems.at[len(copies)]))
        copies[-1].start()

    for f in range(frames):
        send(middle_ref.at[f], out_ref.at[f, 1 : strip - 1])
    edges = ((inner_ref, inner_halo, from_inside, strip - 1), (outer_ref, outer_halo, from_outside, 0))
    for side, (mixed_ref, halo_ref, beyond, row) in enumerate(edges):
        mixed = mixed_ref[...] + beyond(halo_ref, w_ref)
        for f in range(frames):
            ready[side, f] = residual(x_ref[f, place(row, strip)], mixed[f])
            send(ready.at[side, f], out_ref.at[f, place(row, strip)])
    for copy in copies:
        copy.wait()


def call(kernel, out_shape, in_specs, out_specs, scratch, flops, aliases=None):
    return pl.pallas_call(
        kernel,
        out_shape=out_shape,
        in_specs=in_specs,
        out_specs=out_specs,
        scratch_shapes=scratch,
        input_output_aliases=aliases or {},
        compiler_params=pltpu.CompilerParams(vmem_limit_bytes=LIMIT),
        cost_estimate=pl.CostEstimate(flops=flops, bytes_accessed=1 << 20, transcendentals=0),
    )


def swapped(value, axis, distance):
    return lax.ppermute(value, axis, [(i, i ^ distance) for i in range(lax.axis_size(axis))])


def swapped_between(value, lower):
    places, count = lax.axis_size("tm"), lax.axis_size("rows")
    pairs = []
    for place_in in range(places):
        for i in range(count):
            if place_in in (lower, lower + 1):
                pairs.append((place_in * count + i, (2 * lower + 1 - place_in) * count + i))
            else:
                pairs.append((place_in * count + i, place_in * count + (i ^ 1)))
    return lax.ppermute(value, ("tm", "rows"), pairs)


def across_chips(value):
    groups, count = lax.axis_size("groups"), lax.axis_size("rows")
    pairs = []
    for group in range(groups):
        for i in range(count):
            other = (i + 1 if i % 2 else i - 1) % count
            side = group
            if groups % 2 == 0 and i in (0, count - 1):
                other, side = i, group ^ 1
            pairs.append((group * count + i, side * count + other))
    return lax.ppermute(value, ("groups", "rows"), pairs)


def butterfly(value, decay, axis):
    count, mine = lax.axis_size(axis), lax.axis_index(axis)
    total, carried, distance = value, None, 1
    before = jnp.ones_like(decay)
    while distance < count:
        other = swapped(total, axis, distance).astype(F32)
        after = (mine & distance) != 0
        own = total.astype(F32)
        here = jnp.where(after, before * other, 0.0)
        carried = here if carried is None else carried + here
        if 2 * distance < count:
            earlier, later = jnp.where(after, other, own), jnp.where(after, own, other)
            total = (decay * earlier + later).astype(value.dtype)
            before = jnp.where(after, decay * before, before)
            decay = decay * decay
        distance *= 2
    return carried


def local(latents, weight_in, weight_out, decay_table, decay_index):
    frames, strip, width, channels = latents.shape
    shaped = jax.ShapeDtypeStruct
    row, last = (frames, width, channels), (width, channels)
    inside = (strip - 2, width, channels)
    row_f32, row_bf16, last_bf16 = shaped(row, F32), shaped(row, BF16), shaped(last, BF16)
    inside_bf16 = shaped(inside, BF16)
    order = shaped((frames, 1, channels), F32)
    conv_flops = 2 * 9 * frames * strip * width * channels * channels
    taps = pltpu.VMEM((3, frames, strip, width, channels), F32)

    x_outer, x_inner = call(rows_kernel, (row_bf16,) * 2, [VMEM], (VMEM,) * 2, [], 2 * conv_flops)(latents)
    halo_outer = across_chips(x_outer)
    halo_inner = swapped(x_inner, "rows", 1)
    outer, middle, inner, sent, growth = call(
        drive_kernel,
        (row_f32, shaped((frames,) + inside, F32), row_f32, inside_bf16, order),
        [VMEM] * 4,
        (VMEM,) * 5,
        [taps, pltpu.VMEM((strip, width, channels), F32)],
        SMALL,
    )(latents, weight_in, decay_table[None, :], decay_index[None, :])

    def edge(beyond, halo, mixed, growth):
        kernel = functools.partial(drive_edge_kernel, beyond)
        return call(kernel, (row_f32, last_bf16, order), [VMEM] * 4, (VMEM,) * 3, [], SMALL)(halo, weight_in, growth, mixed)

    if lax.axis_size("tm") == 4:
        first = swapped(sent, "tm", 1)
        inner, sent_inner, growth = edge(from_inside, halo_inner, inner, growth)
        outer, sent_outer, growth = edge(from_outside, halo_outer, outer, growth)
        near_outer = swapped(sent_outer, "tm", 1)
        near_inner = swapped(sent_inner, "tm", 1)
        total, growth = call(pair_kernel, (inside_bf16, order), [VMEM] * 3, (VMEM,) * 2, [], SMALL)(sent, first, growth)
        second = swapped_between(total, 1)
        total_outer, growth = call(pair_kernel, (last_bf16, order), [VMEM] * 3, (VMEM,) * 2, [], SMALL)(sent_outer, near_outer, growth)
        far_outer = swapped(total_outer, "tm", 2)
        total_inner, growth = call(pair_kernel, (last_bf16, order), [VMEM] * 3, (VMEM,) * 2, [], LONG)(sent_inner, near_inner, growth)
        far_inner = swapped(total_inner, "tm", 2)
        message, growth = call(relay_kernel, (inside_bf16, order), [VMEM] * 3, (VMEM,) * 2, [], SMALL)(sent, second, growth)
        third = swapped(message, "tm", 1)
        finish_states = call(edge_states_kernel, (row_bf16, order), [VMEM] * 4, (VMEM,) * 2, [], SMALL)
        states_outer, growth = finish_states(outer, near_outer, far_outer, growth)
        halo_outer = across_chips(states_outer)
        states_inner, growth = finish_states(inner, near_inner, far_inner, growth)
        halo_inner = swapped(states_inner, "rows", 1)
        states_middle = call(middle_states_kernel, shaped((frames,) + inside, BF16), [VMEM] * 5, VMEM, [], SMALL)(
            middle, first, second, third, growth
        )
    else:
        inner, sent_inner, growth = edge(from_inside, halo_inner, inner, growth)
        outer, sent_outer, growth = edge(from_outside, halo_outer, outer, growth)
        over = growth[frames - 1]
        states_outer = (outer + growth * butterfly(sent_outer, over, "tm")[None]).astype(BF16)
        states_inner = (inner + growth * butterfly(sent_inner, over, "tm")[None]).astype(BF16)
        states_middle = (middle + growth[:, None] * butterfly(sent, over, "tm")[None]).astype(BF16)
        halo_outer = across_chips(states_outer)
        halo_inner = swapped(states_inner, "rows", 1)

    outer, middle, inner = call(
        mix_kernel,
        (row_f32, shaped((frames,) + inside, BF16), row_f32),
        [VMEM] * 5,
        (VMEM,) * 3,
        [pltpu.VMEM(latents.shape, BF16), taps],
        SMALL,
    )(states_outer, states_middle, states_inner, weight_out, latents)
    return call(
        finish_kernel,
        shaped(latents.shape, BF16),
        [VMEM] * 7,
        ANY,
        [pltpu.VMEM((2,) + row, BF16), pltpu.SemaphoreType.DMA((3 * frames,))],
        SMALL,
    )(halo_outer, halo_inner, weight_out, outer, inner, middle, latents)


def solution(mesh):
    in_specs = (P(("groups", "tm"), "rows", None, None), P(), P(), P(), P())
    out_specs = P(("groups", "tm"), "rows", None, None)
    return jax.shard_map(local, mesh=mesh, in_specs=in_specs, out_specs=out_specs, check_vma=False)
```

```python
import functools

import jax
import jax.numpy as jnp
from jax import lax
from jax.experimental import pallas as pl
from jax.experimental.pallas import tpu as pltpu
from jax.sharding import PartitionSpec as P

VMEM = pl.BlockSpec(memory_space=pltpu.VMEM)
ANY = pl.BlockSpec(memory_space=pl.ANY)
SMALL = 1000
LONG = 3000000000
LIMIT = 24 * 1024 * 1024
F32, BF16 = jnp.float32, jnp.bfloat16


def turned():
    return lax.axis_index("rows") % 2


def place(row, count):
    return jnp.where(turned() == 1, count - 1 - row, row)


def matmul(rows, weight):
    lead, depth = rows.shape[:-1], rows.shape[-1]
    flat = jnp.dot(rows.reshape(-1, depth), weight, preferred_element_type=F32)
    return flat.reshape(*lead, weight.shape[-1])


def join_columns(left, middle, right):
    width = middle.shape[-2]
    axis = middle.ndim - 2
    column = lax.broadcasted_iota(jnp.int32, middle.shape, axis)
    left = jnp.where(column == 0, 0.0, pltpu.roll(left, 1, axis))
    right = jnp.where(column == width - 1, 0.0, pltpu.roll(right, width - 1, axis))
    return left + middle + right


def own_rows(x_ref, w_ref, taps):
    frames, strip = x_ref.shape[:2]
    for q in range(3):
        for f in range(frames):
            taps[q, f] = matmul(x_ref[f], w_ref[1, q])
            taps[q, f, 1:] += matmul(x_ref[f, : strip - 1], w_ref[0, q])
            taps[q, f, : strip - 1] += matmul(x_ref[f, 1:], w_ref[2, q])


def from_outside(halo_ref, w_ref):
    mine, count = lax.axis_index("rows"), lax.axis_size("rows")
    halo = halo_ref[...]
    inside = jnp.logical_and(mine > 0, mine < count - 1)
    halo = jnp.where(inside, halo, jnp.zeros_like(halo))
    return join_columns(*[matmul(halo, w_ref[place(0, 3), q]) for q in range(3)])


def from_inside(halo_ref, w_ref):
    return join_columns(*[matmul(halo_ref[...], w_ref[place(2, 3), q]) for q in range(3)])


def rows_kernel(x_ref, outer_ref, inner_ref):
    frames, strip = x_ref.shape[:2]
    for f in range(frames):
        outer_ref[f] = x_ref[f, place(0, strip)]
        inner_ref[f] = x_ref[f, place(strip - 1, strip)]


def drive_kernel(x_ref, w_ref, table_ref, index_ref, outer_ref, middle_ref, inner_ref, sent_ref, growth_ref, taps, states):
    frames, strip = x_ref.shape[:2]
    own_rows(x_ref, w_ref, taps)
    index = index_ref[...]
    decay = jnp.zeros(index.shape, F32)
    for level in range(table_ref.shape[1]):
        decay = jnp.where(index == level, table_ref[:, level : level + 1], decay)
    growth = decay
    state = None
    for f in range(frames):
        growth_ref[f] = growth
        growth = growth * decay
        driven = join_columns(taps[0, f], taps[1, f], taps[2, f])
        state = driven if state is None else decay.reshape(1, 1, -1) * state + driven
        states[...] = state
        outer_ref[f] = states[place(0, strip)]
        middle_ref[f] = state[1 : strip - 1]
        inner_ref[f] = states[place(strip - 1, strip)]
    sent_ref[...] = state[1 : strip - 1].astype(BF16)


def drive_edge_kernel(beyond, halo_ref, w_ref, growth_ref, row_ref, result_ref, sent_ref, order_ref):
    frames = row_ref.shape[0]
    driven = beyond(halo_ref, w_ref)
    decay = growth_ref[0]
    more = None
    for f in range(frames):
        more = driven[f] if more is None else decay * more + driven[f]
        state = row_ref[f] + more
        result_ref[f] = state
    sent_ref[...] = state.astype(BF16)
    order_ref[...] = growth_ref[...]


def pair_kernel(own_ref, other_ref, growth_ref, total_ref, order_ref):
    over = growth_ref[growth_ref.shape[0] - 1]
    own, other = own_ref[...].astype(F32), other_ref[...].astype(F32)
    after = lax.axis_index("tm") % 2 == 1
    earlier, later = jnp.where(after, other, own), jnp.where(after, own, other)
    total_ref[...] = (over * earlier + later).astype(BF16)
    order_ref[...] = growth_ref[...]


def edge_states_kernel(row_ref, near_ref, far_ref, growth_ref, states_ref, order_ref):
    frames = row_ref.shape[0]
    over = growth_ref[frames - 1]
    mine = lax.axis_index("tm")
    near, far = near_ref[...].astype(F32), far_ref[...].astype(F32)
    far = jnp.where(mine >= 2, far, 0.0)
    carried = jnp.where(mine % 2 == 1, over * far + near, far)
    for f in range(frames):
        states_ref[f] = (row_ref[f] + growth_ref[f] * carried).astype(BF16)
    order_ref[...] = growth_ref[...]


def far_relay_kernel(own_ref, far_ref, growth_ref, message_ref, order_ref):
    over = growth_ref[growth_ref.shape[0] - 1]
    mine = lax.axis_index("tm")
    far = jnp.where(mine >= 2, far_ref[...].astype(F32), 0.0)
    message = jnp.where(mine % 2 == 1, far, over * over * far + own_ref[...].astype(F32))
    message_ref[...] = message.astype(BF16)
    order_ref[...] = growth_ref[...]


def far_states_kernel(row_ref, far_ref, near_ref, growth_ref, states_ref, order_ref):
    frames = row_ref.shape[0]
    mine = lax.axis_index("tm")
    far = jnp.where(mine >= 2, far_ref[...].astype(F32), 0.0)
    near = jnp.where(mine >= 1, near_ref[...].astype(F32), 0.0)
    carried = near + growth_ref[frames - 1] * far
    for f in range(frames):
        states_ref[f] = (row_ref[f] + growth_ref[f] * carried).astype(BF16)
    order_ref[...] = growth_ref[...]


def relay_kernel(own_ref, before_ref, growth_ref, message_ref, order_ref):
    over = growth_ref[growth_ref.shape[0] - 1]
    message_ref[...] = (over * before_ref[...].astype(F32) + own_ref[...].astype(F32)).astype(BF16)
    order_ref[...] = growth_ref[...]


def residual(x, mixed):
    return (x.astype(F32) + jax.nn.gelu(mixed)).astype(BF16)


def mix_ends_kernel(outer_in, inner_in, w_ref, outer_ref, middle_ref, inner_ref):
    frames, inside = middle_ref.shape[:2]
    outer, inner = outer_in[...], inner_in[...]
    first = jnp.where(turned() == 1, inner, outer)
    last = jnp.where(turned() == 1, outer, inner)
    parts = [[[] for _ in range(inside)] for _ in range(3)]
    ends = []
    for q in range(3):
        ends.append(matmul(jnp.concatenate([outer, inner]), w_ref[1, q]))
        parts[q][0].append(matmul(first, w_ref[0, q]))
        parts[q][inside - 1].append(matmul(last, w_ref[2, q]))
    for row in range(inside):
        if parts[0][row]:
            middle_ref[:, row] = join_columns(*[sum(parts[q][row]) for q in range(3)])
        else:
            middle_ref[:, row] = jnp.zeros(first.shape, F32)
    ends = join_columns(*ends)
    outer_ref[...] = ends[:frames]
    inner_ref[...] = ends[frames:]


def mix_inside_kernel(
    first_ref, second_ref, third_ref, growth_ref, states_ref, w_ref, outer_in, middle_in, inner_in, x_ref,
    outer_ref, middle_ref, inner_ref, taps, mixed,
):
    frames, strip = x_ref.shape[:2]
    mine = lax.axis_index("tm")
    carried = third_ref[...].astype(F32)
    for hop, ref in enumerate((first_ref, second_ref)):
        carried = jnp.where(mine == hop + 1, ref[...].astype(F32), carried)
    carried = jnp.where(mine == 0, 0.0, carried)
    states = (states_ref[...] + growth_ref[...][:, None] * carried[None]).astype(BF16)
    for q in range(3):
        above, level, below = (matmul(states, w_ref[tap, q]) for tap in (2, 1, 0))
        for f in range(frames):
            taps[q, f, 1 : strip - 1] = level[f]
            taps[q, f, 0] = above[f, 0]
            taps[q, f, strip - 1] = below[f, strip - 3]
            if strip > 3:
                taps[q, f, 1 : strip - 2] += above[f, 1:]
                taps[q, f, 2 : strip - 1] += below[f, : strip - 3]
    for f in range(frames):
        mixed[...] = join_columns(taps[0, f], taps[1, f], taps[2, f])
        outer_ref[f] = outer_in[f] + mixed[place(0, strip)]
        inner_ref[f] = inner_in[f] + mixed[place(strip - 1, strip)]
        middle_ref[f] = residual(x_ref[f, 1 : strip - 1], middle_in[f] + mixed[1 : strip - 1])


def mix_beyond_kernel(halo_ref, w_ref, outer_in, outer_ref):
    outer_ref[...] = outer_in[...] + from_outside(halo_ref, w_ref)


def finish_kernel(halo_ref, w_ref, outer_ref, inner_ref, middle_ref, x_ref, out_ref, ready, sems):
    frames, strip = x_ref.shape[:2]
    copies = []

    def send(source, target):
        copies.append(pltpu.make_async_copy(source, target, sems.at[len(copies)]))
        copies[-1].start()

    for f in range(frames):
        send(middle_ref.at[f], out_ref.at[f, 1 : strip - 1])
    for side, row in ((0, 0), (1, strip - 1)):
        mixed = inner_ref[...] + from_inside(halo_ref, w_ref) if side else outer_ref[...]
        for f in range(frames):
            ready[side, f] = residual(x_ref[f, place(row, strip)], mixed[f])
            send(ready.at[side, f], out_ref.at[f, place(row, strip)])
    for copy in copies:
        copy.wait()


def call(kernel, out_shape, in_specs, out_specs, scratch, flops, aliases=None):
    return pl.pallas_call(
        kernel,
        out_shape=out_shape,
        in_specs=in_specs,
        out_specs=out_specs,
        scratch_shapes=scratch,
        input_output_aliases=aliases or {},
        compiler_params=pltpu.CompilerParams(vmem_limit_bytes=LIMIT),
        cost_estimate=pl.CostEstimate(flops=flops, bytes_accessed=1 << 20, transcendentals=0),
    )


def swapped(value, axis, distance):
    return lax.ppermute(value, axis, [(i, i ^ distance) for i in range(lax.axis_size(axis))])


def swapped_between(value, lower):
    places, count = lax.axis_size("tm"), lax.axis_size("rows")
    pairs = []
    for place_in in range(places):
        for i in range(count):
            if place_in in (lower, lower + 1):
                pairs.append((place_in * count + i, (2 * lower + 1 - place_in) * count + i))
            else:
                pairs.append((place_in * count + i, place_in * count + (i ^ 1)))
    return lax.ppermute(value, ("tm", "rows"), pairs)


def across_chips(value):
    groups, count = lax.axis_size("groups"), lax.axis_size("rows")
    pairs = []
    for group in range(groups):
        for i in range(count):
            other = (i + 1 if i % 2 else i - 1) % count
            side = group
            if groups % 2 == 0 and i in (0, count - 1):
                other, side = i, group ^ 1
            pairs.append((group * count + i, side * count + other))
    return lax.ppermute(value, ("groups", "rows"), pairs)


def butterfly(value, decay, axis):
    count, mine = lax.axis_size(axis), lax.axis_index(axis)
    total, carried, distance = value, None, 1
    before = jnp.ones_like(decay)
    while distance < count:
        other = swapped(total, axis, distance).astype(F32)
        after = (mine & distance) != 0
        own = total.astype(F32)
        here = jnp.where(after, before * other, 0.0)
        carried = here if carried is None else carried + here
        if 2 * distance < count:
            earlier, later = jnp.where(after, other, own), jnp.where(after, own, other)
            total = (decay * earlier + later).astype(value.dtype)
            before = jnp.where(after, decay * before, before)
            decay = decay * decay
        distance *= 2
    return carried


def local(latents, weight_in, weight_out, decay_table, decay_index):
    frames, strip, width, channels = latents.shape
    shaped = jax.ShapeDtypeStruct
    row, last = (frames, width, channels), (width, channels)
    inside = (strip - 2, width, channels)
    row_f32, row_bf16, last_bf16 = shaped(row, F32), shaped(row, BF16), shaped(last, BF16)
    inside_bf16, middle_f32 = shaped(inside, BF16), shaped((frames,) + inside, F32)
    order = shaped((frames, 1, channels), F32)
    conv_flops = 2 * 9 * frames * strip * width * channels * channels
    taps = pltpu.VMEM((3, frames, strip, width, channels), F32)

    x_outer, x_inner = call(rows_kernel, (row_bf16,) * 2, [VMEM], (VMEM,) * 2, [], 2 * conv_flops)(latents)
    halo_outer = across_chips(x_outer)
    halo_inner = swapped(x_inner, "rows", 1)
    outer, middle, inner, sent, growth = call(
        drive_kernel,
        (row_f32, middle_f32, row_f32, inside_bf16, order),
        [VMEM] * 4,
        (VMEM,) * 5,
        [taps, pltpu.VMEM((strip, width, channels), F32)],
        SMALL,
    )(latents, weight_in, decay_table[None, :], decay_index[None, :])

    def edge(beyond, halo, mixed, growth):
        kernel = functools.partial(drive_edge_kernel, beyond)
        return call(kernel, (row_f32, last_bf16, order), [VMEM] * 4, (VMEM,) * 3, [], SMALL)(halo, weight_in, growth, mixed)

    if lax.axis_size("tm") == 4:
        first = swapped(sent, "tm", 1)
        inner, sent_inner, growth = edge(from_inside, halo_inner, inner, growth)
        outer, sent_outer, growth = edge(from_outside, halo_outer, outer, growth)
        far_outer = swapped(sent_outer, "tm", 2)
        near_inner = swapped(sent_inner, "tm", 1)
        total, growth = call(pair_kernel, (inside_bf16, order), [VMEM] * 3, (VMEM,) * 2, [], SMALL)(sent, first, growth)
        second = swapped_between(total, 1)
        relayed, growth = call(far_relay_kernel, (last_bf16, order), [VMEM] * 3, (VMEM,) * 2, [], SMALL)(sent_outer, far_outer, growth)
        near_outer = swapped(relayed, "tm", 1)
        total_inner, growth = call(pair_kernel, (last_bf16, order), [VMEM] * 3, (VMEM,) * 2, [], LONG)(sent_inner, near_inner, growth)
        far_inner = swapped(total_inner, "tm", 2)
        message, growth = call(relay_kernel, (inside_bf16, order), [VMEM] * 3, (VMEM,) * 2, [], SMALL)(sent, second, growth)
        third = swapped(message, "tm", 1)
        states_outer, growth = call(far_states_kernel, (row_bf16, order), [VMEM] * 4, (VMEM,) * 2, [], SMALL)(
            outer, far_outer, near_outer, growth
        )
        halo_outer = across_chips(states_outer)
        states_inner, growth = call(edge_states_kernel, (row_bf16, order), [VMEM] * 4, (VMEM,) * 2, [], SMALL)(
            inner, near_inner, far_inner, growth
        )
        halo_inner = swapped(states_inner, "rows", 1)
    else:
        inner, sent_inner, growth = edge(from_inside, halo_inner, inner, growth)
        outer, sent_outer, growth = edge(from_outside, halo_outer, outer, growth)
        over = growth[frames - 1]
        states_outer = (outer + growth * butterfly(sent_outer, over, "tm")[None]).astype(BF16)
        states_inner = (inner + growth * butterfly(sent_inner, over, "tm")[None]).astype(BF16)
        first = second = third = butterfly(sent, over, "tm").astype(BF16)
        halo_outer = across_chips(states_outer)
        halo_inner = swapped(states_inner, "rows", 1)

    ends = call(mix_ends_kernel, (row_f32, middle_f32, row_f32), [VMEM] * 3, (VMEM,) * 3, [], SMALL)(
        states_outer, states_inner, weight_out
    )
    outer, middle, inner = call(
        mix_inside_kernel,
        (row_f32, shaped((frames,) + inside, BF16), row_f32),
        [VMEM] * 10,
        (VMEM,) * 3,
        [taps, pltpu.VMEM((strip, width, channels), F32)],
        SMALL,
    )(first, second, third, growth, middle, weight_out, *ends, latents)
    outer = call(mix_beyond_kernel, row_f32, [VMEM] * 3, VMEM, [], SMALL)(halo_outer, weight_out, outer)
    return call(
        finish_kernel,
        shaped(latents.shape, BF16),
        [VMEM] * 6,
        ANY,
        [pltpu.VMEM((2,) + row, BF16), pltpu.SemaphoreType.DMA((3 * frames,))],
        SMALL,
    )(halo_inner, weight_out, outer, inner, middle, latents)


def solution(mesh):
    in_specs = (P(("groups", "tm"), "rows", None, None), P(), P(), P(), P())
    out_specs = P(("groups", "tm"), "rows", None, None)
    return jax.shard_map(local, mesh=mesh, in_specs=in_specs, out_specs=out_specs, check_vma=False)
```

```python
import functools

import jax
import jax.numpy as jnp
from jax import lax
from jax.experimental import pallas as pl
from jax.experimental.pallas import tpu as pltpu
from jax.sharding import PartitionSpec as P

VMEM = pl.BlockSpec(memory_space=pltpu.VMEM)
ANY = pl.BlockSpec(memory_space=pl.ANY)
SMALL = 1000
LONG = 3000000000
LIMIT = 24 * 1024 * 1024
F32, BF16 = jnp.float32, jnp.bfloat16


def turned():
    return lax.axis_index("rows") % 2


def place(row, count):
    return jnp.where(turned() == 1, count - 1 - row, row)


def matmul(rows, weight):
    lead, depth = rows.shape[:-1], rows.shape[-1]
    flat = jnp.dot(rows.reshape(-1, depth), weight, preferred_element_type=F32)
    return flat.reshape(*lead, weight.shape[-1])


def join_columns(left, middle, right):
    width = middle.shape[-2]
    axis = middle.ndim - 2
    column = lax.broadcasted_iota(jnp.int32, middle.shape, axis)
    left = jnp.where(column == 0, 0.0, pltpu.roll(left, 1, axis))
    right = jnp.where(column == width - 1, 0.0, pltpu.roll(right, width - 1, axis))
    return left + middle + right


def own_rows(x_ref, w_ref, taps):
    frames, strip = x_ref.shape[:2]
    for q in range(3):
        for f in range(frames):
            taps[q, f] = matmul(x_ref[f], w_ref[1, q])
            taps[q, f, 1:] += matmul(x_ref[f, : strip - 1], w_ref[0, q])
            taps[q, f, : strip - 1] += matmul(x_ref[f, 1:], w_ref[2, q])


def from_outside(halo_ref, w_ref):
    mine, count = lax.axis_index("rows"), lax.axis_size("rows")
    halo = halo_ref[...]
    inside = jnp.logical_and(mine > 0, mine < count - 1)
    halo = jnp.where(inside, halo, jnp.zeros_like(halo))
    return join_columns(*[matmul(halo, w_ref[place(0, 3), q]) for q in range(3)])


def from_inside(halo_ref, w_ref):
    return join_columns(*[matmul(halo_ref[...], w_ref[place(2, 3), q]) for q in range(3)])


def rows_kernel(x_ref, outer_ref, inner_ref):
    frames, strip = x_ref.shape[:2]
    for f in range(frames):
        outer_ref[f] = x_ref[f, place(0, strip)]
        inner_ref[f] = x_ref[f, place(strip - 1, strip)]


def drive_kernel(x_ref, w_ref, table_ref, index_ref, outer_ref, middle_ref, inner_ref, sent_ref, growth_ref, taps, states):
    frames, strip = x_ref.shape[:2]
    own_rows(x_ref, w_ref, taps)
    index = index_ref[...]
    decay = jnp.zeros(index.shape, F32)
    for level in range(table_ref.shape[1]):
        decay = jnp.where(index == level, table_ref[:, level : level + 1], decay)
    growth = decay
    state = None
    for f in range(frames):
        growth_ref[f] = growth
        growth = growth * decay
        driven = join_columns(taps[0, f], taps[1, f], taps[2, f])
        state = driven if state is None else decay.reshape(1, 1, -1) * state + driven
        states[...] = state
        outer_ref[f] = states[place(0, strip)]
        middle_ref[f] = state[1 : strip - 1]
        inner_ref[f] = states[place(strip - 1, strip)]
    sent_ref[...] = state[1 : strip - 1].astype(BF16)


def drive_edge_kernel(beyond, halo_ref, w_ref, growth_ref, row_ref, result_ref, sent_ref, order_ref):
    frames = row_ref.shape[0]
    driven = beyond(halo_ref, w_ref)
    decay = growth_ref[0]
    more = None
    for f in range(frames):
        more = driven[f] if more is None else decay * more + driven[f]
        state = row_ref[f] + more
        result_ref[f] = state
    sent_ref[...] = state.astype(BF16)
    order_ref[...] = growth_ref[...]


def pair_kernel(own_ref, other_ref, growth_ref, total_ref, order_ref):
    over = growth_ref[growth_ref.shape[0] - 1]
    own, other = own_ref[...].astype(F32), other_ref[...].astype(F32)
    after = lax.axis_index("tm") % 2 == 1
    earlier, later = jnp.where(after, other, own), jnp.where(after, own, other)
    total_ref[...] = (over * earlier + later).astype(BF16)
    order_ref[...] = growth_ref[...]


def edge_states_kernel(row_ref, near_ref, far_ref, growth_ref, states_ref, order_ref):
    frames = row_ref.shape[0]
    over = growth_ref[frames - 1]
    mine = lax.axis_index("tm")
    near, far = near_ref[...].astype(F32), far_ref[...].astype(F32)
    far = jnp.where(mine >= 2, far, 0.0)
    carried = jnp.where(mine % 2 == 1, over * far + near, far)
    for f in range(frames):
        states_ref[f] = (row_ref[f] + growth_ref[f] * carried).astype(BF16)
    order_ref[...] = growth_ref[...]


def far_relay_kernel(own_ref, far_ref, growth_ref, message_ref, order_ref):
    over = growth_ref[growth_ref.shape[0] - 1]
    mine = lax.axis_index("tm")
    far = jnp.where(mine >= 2, far_ref[...].astype(F32), 0.0)
    message = jnp.where(mine % 2 == 1, far, over * over * far + own_ref[...].astype(F32))
    message_ref[...] = message.astype(BF16)
    order_ref[...] = growth_ref[...]


def far_states_kernel(row_ref, far_ref, near_ref, growth_ref, states_ref, order_ref):
    frames = row_ref.shape[0]
    mine = lax.axis_index("tm")
    far = jnp.where(mine >= 2, far_ref[...].astype(F32), 0.0)
    near = jnp.where(mine >= 1, near_ref[...].astype(F32), 0.0)
    carried = near + growth_ref[frames - 1] * far
    for f in range(frames):
        states_ref[f] = (row_ref[f] + growth_ref[f] * carried).astype(BF16)
    order_ref[...] = growth_ref[...]


def relay_kernel(own_ref, before_ref, growth_ref, message_ref, order_ref):
    over = growth_ref[growth_ref.shape[0] - 1]
    message_ref[...] = (over * before_ref[...].astype(F32) + own_ref[...].astype(F32)).astype(BF16)
    order_ref[...] = growth_ref[...]


def residual(x, mixed):
    return (x.astype(F32) + jax.nn.gelu(mixed)).astype(BF16)


def mix_ends_kernel(outer_in, inner_in, w_ref, outer_ref, middle_ref, inner_ref):
    frames, inside = middle_ref.shape[:2]
    outer, inner = outer_in[...], inner_in[...]
    first = jnp.where(turned() == 1, inner, outer)
    last = jnp.where(turned() == 1, outer, inner)
    parts = [[[] for _ in range(inside)] for _ in range(3)]
    ends = []
    for q in range(3):
        ends.append(matmul(jnp.concatenate([outer, inner]), w_ref[1, q]))
        parts[q][0].append(matmul(first, w_ref[0, q]))
        parts[q][inside - 1].append(matmul(last, w_ref[2, q]))
    for row in range(inside):
        if parts[0][row]:
            middle_ref[:, row] = join_columns(*[sum(parts[q][row]) for q in range(3)])
        else:
            middle_ref[:, row] = jnp.zeros(first.shape, F32)
    ends = join_columns(*ends)
    outer_ref[...] = ends[:frames]
    inner_ref[...] = ends[frames:]


def mix_inside_kernel(
    first_ref, second_ref, third_ref, growth_ref, states_ref, w_ref, outer_in, middle_in, inner_in, x_ref,
    outer_ref, middle_ref, inner_ref, taps, mixed,
):
    frames, strip = x_ref.shape[:2]
    mine = lax.axis_index("tm")
    carried = third_ref[...].astype(F32)
    for hop, ref in enumerate((first_ref, second_ref)):
        carried = jnp.where(mine == hop + 1, ref[...].astype(F32), carried)
    carried = jnp.where(mine == 0, 0.0, carried)
    states = (states_ref[...] + growth_ref[...][:, None] * carried[None]).astype(BF16)
    for q in range(3):
        above, level, below = (matmul(states, w_ref[tap, q]) for tap in (2, 1, 0))
        for f in range(frames):
            taps[q, f, 1 : strip - 1] = level[f]
            taps[q, f, 0] = above[f, 0]
            taps[q, f, strip - 1] = below[f, strip - 3]
            if strip > 3:
                taps[q, f, 1 : strip - 2] += above[f, 1:]
                taps[q, f, 2 : strip - 1] += below[f, : strip - 3]
    for f in range(frames):
        mixed[...] = join_columns(taps[0, f], taps[1, f], taps[2, f])
        outer_ref[f] = outer_in[f] + mixed[place(0, strip)]
        inner_ref[f] = inner_in[f] + mixed[place(strip - 1, strip)]
        middle_ref[f] = residual(x_ref[f, 1 : strip - 1], middle_in[f] + mixed[1 : strip - 1])


def mix_beyond_kernel(halo_ref, w_ref, outer_in, outer_ref):
    outer_ref[...] = outer_in[...] + from_outside(halo_ref, w_ref)


def finish_kernel(halo_ref, w_ref, outer_ref, inner_ref, middle_ref, x_ref, out_ref, ready, sems):
    frames, strip = x_ref.shape[:2]
    copies = []

    def send(source, target):
        copies.append(pltpu.make_async_copy(source, target, sems.at[len(copies)]))
        copies[-1].start()

    for f in range(frames):
        send(middle_ref.at[f], out_ref.at[f, 1 : strip - 1])
    for side, row in ((0, 0), (1, strip - 1)):
        mixed = inner_ref[...] + from_inside(halo_ref, w_ref) if side else outer_ref[...]
        for f in range(frames):
            ready[side, f] = residual(x_ref[f, place(row, strip)], mixed[f])
            send(ready.at[side, f], out_ref.at[f, place(row, strip)])
    for copy in copies:
        copy.wait()


def call(kernel, out_shape, in_specs, out_specs, scratch, flops, aliases=None):
    return pl.pallas_call(
        kernel,
        out_shape=out_shape,
        in_specs=in_specs,
        out_specs=out_specs,
        scratch_shapes=scratch,
        input_output_aliases=aliases or {},
        compiler_params=pltpu.CompilerParams(vmem_limit_bytes=LIMIT),
        cost_estimate=pl.CostEstimate(flops=flops, bytes_accessed=1 << 20, transcendentals=0),
    )


def swapped(value, axis, distance):
    return lax.ppermute(value, axis, [(i, i ^ distance) for i in range(lax.axis_size(axis))])


def swapped_between(value, lower):
    places, count = lax.axis_size("tm"), lax.axis_size("rows")
    pairs = []
    for place_in in range(places):
        for i in range(count):
            if place_in in (lower, lower + 1):
                pairs.append((place_in * count + i, (2 * lower + 1 - place_in) * count + i))
            else:
                pairs.append((place_in * count + i, place_in * count + (i ^ 1)))
    return lax.ppermute(value, ("tm", "rows"), pairs)


def across_chips(value):
    groups, count = lax.axis_size("groups"), lax.axis_size("rows")
    pairs = []
    for group in range(groups):
        for i in range(count):
            other = (i + 1 if i % 2 else i - 1) % count
            side = group
            if groups % 2 == 0 and i in (0, count - 1):
                other, side = i, group ^ 1
            pairs.append((group * count + i, side * count + other))
    return lax.ppermute(value, ("groups", "rows"), pairs)


def butterfly(value, decay, axis):
    count, mine = lax.axis_size(axis), lax.axis_index(axis)
    total, carried, distance = value, None, 1
    before = jnp.ones_like(decay)
    while distance < count:
        other = swapped(total, axis, distance).astype(F32)
        after = (mine & distance) != 0
        own = total.astype(F32)
        here = jnp.where(after, before * other, 0.0)
        carried = here if carried is None else carried + here
        if 2 * distance < count:
            earlier, later = jnp.where(after, other, own), jnp.where(after, own, other)
            total = (decay * earlier + later).astype(value.dtype)
            before = jnp.where(after, decay * before, before)
            decay = decay * decay
        distance *= 2
    return carried


def local(latents, weight_in, weight_out, decay_table, decay_index):
    frames, strip, width, channels = latents.shape
    shaped = jax.ShapeDtypeStruct
    row, last = (frames, width, channels), (width, channels)
    inside = (strip - 2, width, channels)
    row_f32, row_bf16, last_bf16 = shaped(row, F32), shaped(row, BF16), shaped(last, BF16)
    inside_bf16, middle_f32 = shaped(inside, BF16), shaped((frames,) + inside, F32)
    order = shaped((frames, 1, channels), F32)
    conv_flops = 2 * 9 * frames * strip * width * channels * channels
    taps = pltpu.VMEM((3, frames, strip, width, channels), F32)

    x_outer, x_inner = call(rows_kernel, (row_bf16,) * 2, [VMEM], (VMEM,) * 2, [], 2 * conv_flops)(latents)
    halo_outer = across_chips(x_outer)
    halo_inner = swapped(x_inner, "rows", 1)
    outer, middle, inner, sent, growth = call(
        drive_kernel,
        (row_f32, middle_f32, row_f32, inside_bf16, order),
        [VMEM] * 4,
        (VMEM,) * 5,
        [taps, pltpu.VMEM((strip, width, channels), F32)],
        SMALL,
    )(latents, weight_in, decay_table[None, :], decay_index[None, :])

    def edge(beyond, halo, mixed, growth):
        kernel = functools.partial(drive_edge_kernel, beyond)
        return call(kernel, (row_f32, last_bf16, order), [VMEM] * 4, (VMEM,) * 3, [], SMALL)(halo, weight_in, growth, mixed)

    if lax.axis_size("tm") == 4:
        first = swapped_between(sent, 0)
        inner, sent_inner, growth = edge(from_inside, halo_inner, inner, growth)
        outer, sent_outer, growth = edge(from_outside, halo_outer, outer, growth)
        far_outer = swapped(sent_outer, "tm", 2)
        near_inner = swapped(sent_inner, "tm", 1)
        total, growth = call(pair_kernel, (inside_bf16, order), [VMEM] * 3, (VMEM,) * 2, [], SMALL)(sent, first, growth)
        second = swapped_between(total, 1)
        relayed, growth = call(far_relay_kernel, (last_bf16, order), [VMEM] * 3, (VMEM,) * 2, [], SMALL)(sent_outer, far_outer, growth)
        near_outer = swapped(relayed, "tm", 1)
        total_inner, growth = call(pair_kernel, (last_bf16, order), [VMEM] * 3, (VMEM,) * 2, [], LONG)(sent_inner, near_inner, growth)
        far_inner = swapped(total_inner, "tm", 2)
        message, growth = call(relay_kernel, (inside_bf16, order), [VMEM] * 3, (VMEM,) * 2, [], SMALL)(sent, second, growth)
        third = swapped_between(message, 2)
        states_outer, growth = call(far_states_kernel, (row_bf16, order), [VMEM] * 4, (VMEM,) * 2, [], SMALL)(
            outer, far_outer, near_outer, growth
        )
        halo_outer = across_chips(states_outer)
        states_inner, growth = call(edge_states_kernel, (row_bf16, order), [VMEM] * 4, (VMEM,) * 2, [], SMALL)(
            inner, near_inner, far_inner, growth
        )
        halo_inner = swapped(states_inner, "rows", 1)
    else:
        inner, sent_inner, growth = edge(from_inside, halo_inner, inner, growth)
        outer, sent_outer, growth = edge(from_outside, halo_outer, outer, growth)
        over = growth[frames - 1]
        states_outer = (outer + growth * butterfly(sent_outer, over, "tm")[None]).astype(BF16)
        states_inner = (inner + growth * butterfly(sent_inner, over, "tm")[None]).astype(BF16)
        first = second = third = butterfly(sent, over, "tm").astype(BF16)
        halo_outer = across_chips(states_outer)
        halo_inner = swapped(states_inner, "rows", 1)

    ends = call(mix_ends_kernel, (row_f32, middle_f32, row_f32), [VMEM] * 3, (VMEM,) * 3, [], SMALL)(
        states_outer, states_inner, weight_out
    )
    outer, middle, inner = call(
        mix_inside_kernel,
        (row_f32, shaped((frames,) + inside, BF16), row_f32),
        [VMEM] * 10,
        (VMEM,) * 3,
        [taps, pltpu.VMEM((strip, width, channels), F32)],
        SMALL,
    )(first, second, third, growth, middle, weight_out, *ends, latents)
    outer = call(mix_beyond_kernel, row_f32, [VMEM] * 3, VMEM, [], SMALL)(halo_outer, weight_out, outer)
    return call(
        finish_kernel,
        shaped(latents.shape, BF16),
        [VMEM] * 6,
        ANY,
        [pltpu.VMEM((2,) + row, BF16), pltpu.SemaphoreType.DMA((3 * frames,))],
        SMALL,
    )(halo_inner, weight_out, outer, inner, middle, latents)


def solution(mesh):
    in_specs = (P(("groups", "tm"), "rows", None, None), P(), P(), P(), P())
    out_specs = P(("groups", "tm"), "rows", None, None)
    return jax.shard_map(local, mesh=mesh, in_specs=in_specs, out_specs=out_specs, check_vma=False)
```

```python
import functools

import jax
import jax.numpy as jnp
from jax import lax
from jax.experimental import pallas as pl
from jax.experimental.pallas import tpu as pltpu
from jax.sharding import PartitionSpec as P

VMEM = pl.BlockSpec(memory_space=pltpu.VMEM)
ANY = pl.BlockSpec(memory_space=pl.ANY)
SMALL = 1000
LONG = 3000000000
LIMIT = 24 * 1024 * 1024
F32, BF16 = jnp.float32, jnp.bfloat16


def turned():
    return lax.axis_index("rows") % 2


def place(row, count):
    return jnp.where(turned() == 1, count - 1 - row, row)


def matmul(rows, weight):
    lead, depth = rows.shape[:-1], rows.shape[-1]
    flat = jnp.dot(rows.reshape(-1, depth), weight, preferred_element_type=F32)
    return flat.reshape(*lead, weight.shape[-1])


def join_columns(left, middle, right):
    width = middle.shape[-2]
    axis = middle.ndim - 2
    column = lax.broadcasted_iota(jnp.int32, middle.shape, axis)
    left = jnp.where(column == 0, 0.0, pltpu.roll(left, 1, axis))
    right = jnp.where(column == width - 1, 0.0, pltpu.roll(right, width - 1, axis))
    return left + middle + right


def own_rows(x_ref, w_ref, taps):
    frames, strip = x_ref.shape[:2]
    for q in range(3):
        for f in range(frames):
            taps[q, f] = matmul(x_ref[f], w_ref[1, q])
            taps[q, f, 1:] += matmul(x_ref[f, : strip - 1], w_ref[0, q])
            taps[q, f, : strip - 1] += matmul(x_ref[f, 1:], w_ref[2, q])


def from_outside(halo_ref, w_ref):
    mine, count = lax.axis_index("rows"), lax.axis_size("rows")
    halo = halo_ref[...]
    inside = jnp.logical_and(mine > 0, mine < count - 1)
    halo = jnp.where(inside, halo, jnp.zeros_like(halo))
    return join_columns(*[matmul(halo, w_ref[place(0, 3), q]) for q in range(3)])


def from_inside(halo_ref, w_ref):
    return join_columns(*[matmul(halo_ref[...], w_ref[place(2, 3), q]) for q in range(3)])


def rows_kernel(x_ref, outer_ref, inner_ref):
    frames, strip = x_ref.shape[:2]
    for f in range(frames):
        outer_ref[f] = x_ref[f, place(0, strip)]
        inner_ref[f] = x_ref[f, place(strip - 1, strip)]


def drive_kernel(x_ref, w_ref, table_ref, index_ref, outer_ref, middle_ref, inner_ref, sent_ref, growth_ref, taps, states):
    frames, strip = x_ref.shape[:2]
    own_rows(x_ref, w_ref, taps)
    index = index_ref[...]
    decay = jnp.zeros(index.shape, F32)
    for level in range(table_ref.shape[1]):
        decay = jnp.where(index == level, table_ref[:, level : level + 1], decay)
    growth = decay
    state = None
    for f in range(frames):
        growth_ref[f] = growth
        growth = growth * decay
        driven = join_columns(taps[0, f], taps[1, f], taps[2, f])
        state = driven if state is None else decay.reshape(1, 1, -1) * state + driven
        states[...] = state
        outer_ref[f] = states[place(0, strip)]
        middle_ref[f] = state[1 : strip - 1]
        inner_ref[f] = states[place(strip - 1, strip)]
    sent_ref[...] = state[1 : strip - 1].astype(BF16)


def drive_edge_kernel(beyond, halo_ref, w_ref, growth_ref, row_ref, result_ref, sent_ref, order_ref):
    frames = row_ref.shape[0]
    driven = beyond(halo_ref, w_ref)
    decay = growth_ref[0]
    more = None
    for f in range(frames):
        more = driven[f] if more is None else decay * more + driven[f]
        state = row_ref[f] + more
        result_ref[f] = state
    sent_ref[...] = state.astype(BF16)
    order_ref[...] = growth_ref[...]


def pair_kernel(own_ref, other_ref, growth_ref, total_ref, order_ref):
    over = growth_ref[growth_ref.shape[0] - 1]
    own, other = own_ref[...].astype(F32), other_ref[...].astype(F32)
    after = lax.axis_index("tm") % 2 == 1
    earlier, later = jnp.where(after, other, own), jnp.where(after, own, other)
    total_ref[...] = (over * earlier + later).astype(BF16)
    order_ref[...] = growth_ref[...]


def edge_states_kernel(row_ref, near_ref, far_ref, growth_ref, states_ref, order_ref):
    frames = row_ref.shape[0]
    over = growth_ref[frames - 1]
    mine = lax.axis_index("tm")
    near, far = near_ref[...].astype(F32), far_ref[...].astype(F32)
    far = jnp.where(mine >= 2, far, 0.0)
    carried = jnp.where(mine % 2 == 1, over * far + near, far)
    for f in range(frames):
        states_ref[f] = (row_ref[f] + growth_ref[f] * carried).astype(BF16)
    order_ref[...] = growth_ref[...]


def by_hop(first_ref, second_ref, third_ref):
    mine = lax.axis_index("tm")
    carried = third_ref[...].astype(F32)
    for hop, ref in enumerate((first_ref, second_ref)):
        carried = jnp.where(mine == hop + 1, ref[...].astype(F32), carried)
    return jnp.where(mine == 0, 0.0, carried)


def far_relay_kernel(own_ref, far_ref, growth_ref, message_ref, order_ref):
    over = growth_ref[growth_ref.shape[0] - 1]
    mine = lax.axis_index("tm")
    far = jnp.where(mine >= 2, far_ref[...].astype(F32), 0.0)
    message = jnp.where(mine % 2 == 1, far, over * over * far + own_ref[...].astype(F32))
    message_ref[...] = message.astype(BF16)
    order_ref[...] = growth_ref[...]


def far_states_kernel(row_ref, far_ref, near_ref, growth_ref, states_ref, order_ref):
    frames = row_ref.shape[0]
    mine = lax.axis_index("tm")
    far = jnp.where(mine >= 2, far_ref[...].astype(F32), 0.0)
    near = jnp.where(mine >= 1, near_ref[...].astype(F32), 0.0)
    carried = near + growth_ref[frames - 1] * far
    for f in range(frames):
        states_ref[f] = (row_ref[f] + growth_ref[f] * carried).astype(BF16)
    order_ref[...] = growth_ref[...]


def relay_kernel(own_ref, before_ref, growth_ref, message_ref, order_ref):
    over = growth_ref[growth_ref.shape[0] - 1]
    message_ref[...] = (over * before_ref[...].astype(F32) + own_ref[...].astype(F32)).astype(BF16)
    order_ref[...] = growth_ref[...]


def residual(x, mixed):
    return (x.astype(F32) + jax.nn.gelu(mixed)).astype(BF16)


def mix_ends_kernel(outer_in, inner_in, w_ref, outer_ref, middle_ref, inner_ref):
    frames, inside = middle_ref.shape[:2]
    outer, inner = outer_in[...], inner_in[...]
    first = jnp.where(turned() == 1, inner, outer)
    last = jnp.where(turned() == 1, outer, inner)
    parts = [[[] for _ in range(inside)] for _ in range(3)]
    ends = []
    for q in range(3):
        ends.append(matmul(jnp.concatenate([outer, inner]), w_ref[1, q]))
        parts[q][0].append(matmul(first, w_ref[0, q]))
        parts[q][inside - 1].append(matmul(last, w_ref[2, q]))
    for row in range(inside):
        if parts[0][row]:
            middle_ref[:, row] = join_columns(*[sum(parts[q][row]) for q in range(3)])
        else:
            middle_ref[:, row] = jnp.zeros(first.shape, F32)
    ends = join_columns(*ends)
    outer_ref[...] = ends[:frames]
    inner_ref[...] = ends[frames:]


def mix_inside_kernel(
    first_ref, second_ref, third_ref, growth_ref, states_ref, w_ref, outer_in, middle_in, inner_in, x_ref,
    outer_ref, middle_ref, inner_ref, taps, mixed,
):
    frames, strip = x_ref.shape[:2]
    mine = lax.axis_index("tm")
    carried = third_ref[...].astype(F32)
    for hop, ref in enumerate((first_ref, second_ref)):
        carried = jnp.where(mine == hop + 1, ref[...].astype(F32), carried)
    carried = jnp.where(mine == 0, 0.0, carried)
    states = (states_ref[...] + growth_ref[...][:, None] * carried[None]).astype(BF16)
    for q in range(3):
        above, level, below = (matmul(states, w_ref[tap, q]) for tap in (2, 1, 0))
        for f in range(frames):
            taps[q, f, 1 : strip - 1] = level[f]
            taps[q, f, 0] = above[f, 0]
            taps[q, f, strip - 1] = below[f, strip - 3]
            if strip > 3:
                taps[q, f, 1 : strip - 2] += above[f, 1:]
                taps[q, f, 2 : strip - 1] += below[f, : strip - 3]
    for f in range(frames):
        mixed[...] = join_columns(taps[0, f], taps[1, f], taps[2, f])
        outer_ref[f] = outer_in[f] + mixed[place(0, strip)]
        inner_ref[f] = inner_in[f] + mixed[place(strip - 1, strip)]
        middle_ref[f] = residual(x_ref[f, 1 : strip - 1], middle_in[f] + mixed[1 : strip - 1])


def mix_beyond_kernel(halo_ref, w_ref, outer_in, outer_ref):
    outer_ref[...] = outer_in[...] + from_outside(halo_ref, w_ref)


def finish_kernel(halo_ref, w_ref, outer_ref, inner_ref, middle_ref, x_ref, out_ref, ready, sems):
    frames, strip = x_ref.shape[:2]
    copies = []

    def send(source, target):
        copies.append(pltpu.make_async_copy(source, target, sems.at[len(copies)]))
        copies[-1].start()

    for f in range(frames):
        send(middle_ref.at[f], out_ref.at[f, 1 : strip - 1])
    for side, row in ((0, 0), (1, strip - 1)):
        mixed = inner_ref[...] + from_inside(halo_ref, w_ref) if side else outer_ref[...]
        for f in range(frames):
            ready[side, f] = residual(x_ref[f, place(row, strip)], mixed[f])
            send(ready.at[side, f], out_ref.at[f, place(row, strip)])
    for copy in copies:
        copy.wait()


def call(kernel, out_shape, in_specs, out_specs, scratch, flops, aliases=None):
    return pl.pallas_call(
        kernel,
        out_shape=out_shape,
        in_specs=in_specs,
        out_specs=out_specs,
        scratch_shapes=scratch,
        input_output_aliases=aliases or {},
        compiler_params=pltpu.CompilerParams(vmem_limit_bytes=LIMIT),
        cost_estimate=pl.CostEstimate(flops=flops, bytes_accessed=1 << 20, transcendentals=0),
    )


def swapped(value, axis, distance):
    return lax.ppermute(value, axis, [(i, i ^ distance) for i in range(lax.axis_size(axis))])


def swapped_between(value, lower):
    places, count = lax.axis_size("tm"), lax.axis_size("rows")
    pairs = []
    for place_in in range(places):
        for i in range(count):
            if place_in in (lower, lower + 1):
                pairs.append((place_in * count + i, (2 * lower + 1 - place_in) * count + i))
            else:
                pairs.append((place_in * count + i, place_in * count + (i ^ 1)))
    return lax.ppermute(value, ("tm", "rows"), pairs)


def across_chips(value):
    groups, count = lax.axis_size("groups"), lax.axis_size("rows")
    pairs = []
    for group in range(groups):
        for i in range(count):
            other = (i + 1 if i % 2 else i - 1) % count
            side = group
            if groups % 2 == 0 and i in (0, count - 1):
                other, side = i, group ^ 1
            pairs.append((group * count + i, side * count + other))
    return lax.ppermute(value, ("groups", "rows"), pairs)


def butterfly(value, decay, axis):
    count, mine = lax.axis_size(axis), lax.axis_index(axis)
    total, carried, distance = value, None, 1
    before = jnp.ones_like(decay)
    while distance < count:
        other = swapped(total, axis, distance).astype(F32)
        after = (mine & distance) != 0
        own = total.astype(F32)
        here = jnp.where(after, before * other, 0.0)
        carried = here if carried is None else carried + here
        if 2 * distance < count:
            earlier, later = jnp.where(after, other, own), jnp.where(after, own, other)
            total = (decay * earlier + later).astype(value.dtype)
            before = jnp.where(after, decay * before, before)
            decay = decay * decay
        distance *= 2
    return carried


def local(latents, weight_in, weight_out, decay_table, decay_index):
    frames, strip, width, channels = latents.shape
    shaped = jax.ShapeDtypeStruct
    row, last = (frames, width, channels), (width, channels)
    inside = (strip - 2, width, channels)
    row_f32, row_bf16, last_bf16 = shaped(row, F32), shaped(row, BF16), shaped(last, BF16)
    inside_bf16, middle_f32 = shaped(inside, BF16), shaped((frames,) + inside, F32)
    order = shaped((frames, 1, channels), F32)
    conv_flops = 2 * 9 * frames * strip * width * channels * channels
    taps = pltpu.VMEM((3, frames, strip, width, channels), F32)

    x_outer, x_inner = call(rows_kernel, (row_bf16,) * 2, [VMEM], (VMEM,) * 2, [], 2 * conv_flops)(latents)
    halo_outer = across_chips(x_outer)
    halo_inner = swapped(x_inner, "rows", 1)
    outer, middle, inner, sent, growth = call(
        drive_kernel,
        (row_f32, middle_f32, row_f32, inside_bf16, order),
        [VMEM] * 4,
        (VMEM,) * 5,
        [taps, pltpu.VMEM((strip, width, channels), F32)],
        SMALL,
    )(latents, weight_in, decay_table[None, :], decay_index[None, :])

    def edge(beyond, halo, mixed, growth):
        kernel = functools.partial(drive_edge_kernel, beyond)
        return call(kernel, (row_f32, last_bf16, order), [VMEM] * 4, (VMEM,) * 3, [], SMALL)(halo, weight_in, growth, mixed)

    if lax.axis_size("tm") == 4:
        first = swapped_between(sent, 0)
        outer, sent_outer, growth = edge(from_outside, halo_outer, outer, growth)
        inner, sent_inner, growth = edge(from_inside, halo_inner, inner, growth)
        far_outer = swapped(sent_outer, "tm", 2)
        near_inner = swapped(sent_inner, "tm", 1)
        total, growth = call(relay_kernel, (inside_bf16, order), [VMEM] * 3, (VMEM,) * 2, [], SMALL)(sent, first, growth)
        second = swapped_between(total, 1)
        relayed_outer, growth = call(far_relay_kernel, (last_bf16, order), [VMEM] * 3, (VMEM,) * 2, [], LONG)(sent_outer, far_outer, growth)
        near_outer = swapped(relayed_outer, "tm", 1)
        total_inner, growth = call(pair_kernel, (last_bf16, order), [VMEM] * 3, (VMEM,) * 2, [], LONG)(sent_inner, near_inner, growth)
        far_inner = swapped(total_inner, "tm", 2)
        message, growth = call(relay_kernel, (inside_bf16, order), [VMEM] * 3, (VMEM,) * 2, [], SMALL)(sent, second, growth)
        third = swapped_between(message, 2)
        states_outer, growth = call(far_states_kernel, (row_bf16, order), [VMEM] * 4, (VMEM,) * 2, [], SMALL)(outer, far_outer, near_outer, growth)
        halo_outer = across_chips(states_outer)
        states_inner, growth = call(edge_states_kernel, (row_bf16, order), [VMEM] * 4, (VMEM,) * 2, [], SMALL)(inner, near_inner, far_inner, growth)
        halo_inner = swapped(states_inner, "rows", 1)
    else:
        inner, sent_inner, growth = edge(from_inside, halo_inner, inner, growth)
        outer, sent_outer, growth = edge(from_outside, halo_outer, outer, growth)
        over = growth[frames - 1]
        states_outer = (outer + growth * butterfly(sent_outer, over, "tm")[None]).astype(BF16)
        states_inner = (inner + growth * butterfly(sent_inner, over, "tm")[None]).astype(BF16)
        first = second = third = butterfly(sent, over, "tm").astype(BF16)
        halo_outer = across_chips(states_outer)
        halo_inner = swapped(states_inner, "rows", 1)

    ends = call(mix_ends_kernel, (row_f32, middle_f32, row_f32), [VMEM] * 3, (VMEM,) * 3, [], SMALL)(
        states_outer, states_inner, weight_out
    )
    outer, middle, inner = call(
        mix_inside_kernel,
        (row_f32, shaped((frames,) + inside, BF16), row_f32),
        [VMEM] * 10,
        (VMEM,) * 3,
        [taps, pltpu.VMEM((strip, width, channels), F32)],
        SMALL,
    )(first, second, third, growth, middle, weight_out, *ends, latents)
    outer = call(mix_beyond_kernel, row_f32, [VMEM] * 3, VMEM, [], SMALL)(halo_outer, weight_out, outer)
    return call(
        finish_kernel,
        shaped(latents.shape, BF16),
        [VMEM] * 6,
        ANY,
        [pltpu.VMEM((2,) + row, BF16), pltpu.SemaphoreType.DMA((3 * frames,))],
        SMALL,
    )(halo_inner, weight_out, outer, inner, middle, latents)


def solution(mesh):
    in_specs = (P(("groups", "tm"), "rows", None, None), P(), P(), P(), P())
    out_specs = P(("groups", "tm"), "rows", None, None)
    return jax.shard_map(local, mesh=mesh, in_specs=in_specs, out_specs=out_specs, check_vma=False)
```

```python
import functools

import jax
import jax.numpy as jnp
from jax import lax
from jax.experimental import pallas as pl
from jax.experimental.pallas import tpu as pltpu
from jax.sharding import PartitionSpec as P

VMEM = pl.BlockSpec(memory_space=pltpu.VMEM)
ANY = pl.BlockSpec(memory_space=pl.ANY)
SMALL = 1000
LONG = 3000000000
LIMIT = 24 * 1024 * 1024
F32, BF16 = jnp.float32, jnp.bfloat16


def turned():
    return lax.axis_index("rows") % 2


def place(row, count):
    return jnp.where(turned() == 1, count - 1 - row, row)


def matmul(rows, weight):
    lead, depth = rows.shape[:-1], rows.shape[-1]
    flat = jnp.dot(rows.reshape(-1, depth), weight, preferred_element_type=F32)
    return flat.reshape(*lead, weight.shape[-1])


def join_columns(left, middle, right):
    width = middle.shape[-2]
    axis = middle.ndim - 2
    column = lax.broadcasted_iota(jnp.int32, middle.shape, axis)
    left = jnp.where(column == 0, 0.0, pltpu.roll(left, 1, axis))
    right = jnp.where(column == width - 1, 0.0, pltpu.roll(right, width - 1, axis))
    return left + middle + right


def own_rows(x_ref, w_ref, taps):
    frames, strip = x_ref.shape[:2]
    for q in range(3):
        for f in range(frames):
            taps[q, f] = matmul(x_ref[f], w_ref[1, q])
            taps[q, f, 1:] += matmul(x_ref[f, : strip - 1], w_ref[0, q])
            taps[q, f, : strip - 1] += matmul(x_ref[f, 1:], w_ref[2, q])


def from_outside(halo_ref, w_ref):
    mine, count = lax.axis_index("rows"), lax.axis_size("rows")
    halo = halo_ref[...]
    inside = jnp.logical_and(mine > 0, mine < count - 1)
    halo = jnp.where(inside, halo, jnp.zeros_like(halo))
    return join_columns(*[matmul(halo, w_ref[place(0, 3), q]) for q in range(3)])


def from_inside(halo_ref, w_ref):
    return join_columns(*[matmul(halo_ref[...], w_ref[place(2, 3), q]) for q in range(3)])


def rows_kernel(x_ref, outer_ref, second_ref, inner_ref):
    frames, strip = x_ref.shape[:2]
    for f in range(frames):
        second_ref[f] = x_ref[f, place(1, strip)]
        outer_ref[f] = x_ref[f, place(0, strip)]
        inner_ref[f] = x_ref[f, place(strip - 1, strip)]


def drive_kernel(x_ref, w_ref, table_ref, index_ref, outer_ref, middle_ref, inner_ref, sent_ref, growth_ref, taps, states):
    frames, strip = x_ref.shape[:2]
    own_rows(x_ref, w_ref, taps)
    index = index_ref[...]
    decay = jnp.zeros(index.shape, F32)
    for level in range(table_ref.shape[1]):
        decay = jnp.where(index == level, table_ref[:, level : level + 1], decay)
    growth = decay
    state = None
    for f in range(frames):
        growth_ref[f] = growth
        growth = growth * decay
        driven = join_columns(taps[0, f], taps[1, f], taps[2, f])
        state = driven if state is None else decay.reshape(1, 1, -1) * state + driven
        states[...] = state
        outer_ref[f] = states[place(0, strip)]
        middle_ref[f] = state[1 : strip - 1]
        inner_ref[f] = states[place(strip - 1, strip)]
    sent_ref[...] = state[1 : strip - 1].astype(BF16)


def drive_edge_kernel(beyond, halo_ref, w_ref, growth_ref, row_ref, result_ref, sent_ref, order_ref, *rounded_ref):
    frames = row_ref.shape[0]
    driven = beyond(halo_ref, w_ref)
    decay = growth_ref[0]
    more = None
    for f in range(frames):
        more = driven[f] if more is None else decay * more + driven[f]
        state = row_ref[f] + more
        result_ref[f] = state
        for ref in rounded_ref:
            ref[f] = state.astype(BF16)
    sent_ref[...] = state.astype(BF16)
    order_ref[...] = growth_ref[...]


def later_kernel(x_ref, growth_ref, out_ref):
    out_ref[...] = x_ref[...]


def arrived_kernel(halo_ref, growth_ref, order_ref):
    order_ref[...] = growth_ref[...]


def beyond_states_kernel(second_ref, halo_ref, outer_ref, w_ref, growth_ref, result_ref, order_ref):
    above, level, below = second_ref[...], halo_ref[...], outer_ref[...]
    driven = join_columns(
        *[
            matmul(above, w_ref[place(0, 3), q]) + matmul(level, w_ref[1, q]) + matmul(below, w_ref[place(2, 3), q])
            for q in range(3)
        ]
    )
    state = None
    for f in range(driven.shape[0]):
        state = driven[f] if state is None else growth_ref[0] * state + driven[f]
        result_ref[f] = state
    order_ref[...] = growth_ref[...]


def pair_kernel(own_ref, other_ref, growth_ref, total_ref, order_ref):
    over = growth_ref[growth_ref.shape[0] - 1]
    own, other = own_ref[...].astype(F32), other_ref[...].astype(F32)
    after = lax.axis_index("tm") % 2 == 1
    earlier, later = jnp.where(after, other, own), jnp.where(after, own, other)
    total_ref[...] = (over * earlier + later).astype(BF16)
    order_ref[...] = growth_ref[...]


def edge_states_kernel(row_ref, near_ref, far_ref, growth_ref, states_ref, order_ref, carried_ref):
    frames = row_ref.shape[0]
    over = growth_ref[frames - 1]
    mine = lax.axis_index("tm")
    near, far = near_ref[...].astype(F32), far_ref[...].astype(F32)
    far = jnp.where(mine >= 2, far, 0.0)
    carried = jnp.where(mine % 2 == 1, over * far + near, far)
    carried_ref[...] = carried.astype(BF16)
    for f in range(frames):
        states_ref[f] = (row_ref[f] + growth_ref[f] * carried).astype(BF16)
    order_ref[...] = growth_ref[...]


def by_hop(first_ref, second_ref, third_ref):
    mine = lax.axis_index("tm")
    carried = third_ref[...].astype(F32)
    for hop, ref in enumerate((first_ref, second_ref)):
        carried = jnp.where(mine == hop + 1, ref[...].astype(F32), carried)
    return jnp.where(mine == 0, 0.0, carried)


def far_relay_kernel(own_ref, far_ref, growth_ref, message_ref, order_ref):
    over = growth_ref[growth_ref.shape[0] - 1]
    mine = lax.axis_index("tm")
    far = jnp.where(mine >= 2, far_ref[...].astype(F32), 0.0)
    message = jnp.where(mine % 2 == 1, far, over * over * far + own_ref[...].astype(F32))
    message_ref[...] = message.astype(BF16)
    order_ref[...] = growth_ref[...]


def far_states_kernel(row_ref, far_ref, near_ref, growth_ref, states_ref, order_ref, carried_ref):
    frames = row_ref.shape[0]
    mine = lax.axis_index("tm")
    far = jnp.where(mine >= 2, far_ref[...].astype(F32), 0.0)
    near = jnp.where(mine >= 1, near_ref[...].astype(F32), 0.0)
    carried = near + growth_ref[frames - 1] * far
    carried_ref[...] = carried.astype(BF16)
    for f in range(frames):
        states_ref[f] = (row_ref[f] + growth_ref[f] * carried).astype(BF16)
    order_ref[...] = growth_ref[...]


def relay_kernel(own_ref, before_ref, growth_ref, message_ref, order_ref):
    over = growth_ref[growth_ref.shape[0] - 1]
    message_ref[...] = (over * before_ref[...].astype(F32) + own_ref[...].astype(F32)).astype(BF16)
    order_ref[...] = growth_ref[...]


def residual(x, mixed):
    return (x.astype(F32) + jax.nn.gelu(mixed)).astype(BF16)


def mix_ends_kernel(outer_in, inner_in, w_ref, outer_ref, middle_ref, inner_ref):
    frames, inside = middle_ref.shape[:2]
    outer, inner = outer_in[...], inner_in[...]
    first = jnp.where(turned() == 1, inner, outer)
    last = jnp.where(turned() == 1, outer, inner)
    parts = [[[] for _ in range(inside)] for _ in range(3)]
    ends = []
    for q in range(3):
        ends.append(matmul(jnp.concatenate([outer, inner]), w_ref[1, q]))
        parts[q][0].append(matmul(first, w_ref[0, q]))
        parts[q][inside - 1].append(matmul(last, w_ref[2, q]))
    for row in range(inside):
        if parts[0][row]:
            middle_ref[:, row] = join_columns(*[sum(parts[q][row]) for q in range(3)])
        else:
            middle_ref[:, row] = jnp.zeros(first.shape, F32)
    ends = join_columns(*ends)
    outer_ref[...] = ends[:frames]
    inner_ref[...] = ends[frames:]


def mix_inside_kernel(
    first_ref, second_ref, third_ref, growth_ref, states_ref, w_ref, outer_in, middle_in, inner_in, x_ref,
    outer_ref, middle_ref, inner_ref, taps, mixed,
):
    frames, strip = x_ref.shape[:2]
    mine = lax.axis_index("tm")
    carried = third_ref[...].astype(F32)
    for hop, ref in enumerate((first_ref, second_ref)):
        carried = jnp.where(mine == hop + 1, ref[...].astype(F32), carried)
    carried = jnp.where(mine == 0, 0.0, carried)
    states = (states_ref[...] + growth_ref[...][:, None] * carried[None]).astype(BF16)
    for q in range(3):
        above, level, below = (matmul(states, w_ref[tap, q]) for tap in (2, 1, 0))
        for f in range(frames):
            taps[q, f, 1 : strip - 1] = level[f]
            taps[q, f, 0] = above[f, 0]
            taps[q, f, strip - 1] = below[f, strip - 3]
            if strip > 3:
                taps[q, f, 1 : strip - 2] += above[f, 1:]
                taps[q, f, 2 : strip - 1] += below[f, : strip - 3]
    for f in range(frames):
        mixed[...] = join_columns(taps[0, f], taps[1, f], taps[2, f])
        outer_ref[f] = outer_in[f] + mixed[place(0, strip)]
        inner_ref[f] = inner_in[f] + mixed[place(strip - 1, strip)]
        middle_ref[f] = residual(x_ref[f, 1 : strip - 1], middle_in[f] + mixed[1 : strip - 1])


def carried_on(partial_ref, carried_ref, growth_ref):
    return (partial_ref[...].astype(F32) + growth_ref[...] * carried_ref[...].astype(F32)[None]).astype(BF16)


def mix_beyond_kernel(partial_ref, carried_ref, growth_ref, w_ref, outer_in, outer_ref):
    outer_ref[...] = outer_in[...] + from_outside(carried_on(partial_ref, carried_ref, growth_ref), w_ref)


def finish_kernel(partial_ref, carried_ref, growth_ref, w_ref, outer_ref, inner_ref, middle_ref, x_ref, out_ref, ready, sems):
    frames, strip = x_ref.shape[:2]
    copies = []

    def send(source, target):
        copies.append(pltpu.make_async_copy(source, target, sems.at[len(copies)]))
        copies[-1].start()

    for f in range(frames):
        send(middle_ref.at[f], out_ref.at[f, 1 : strip - 1])
    for side, row in ((0, 0), (1, strip - 1)):
        mixed = inner_ref[...] + from_inside(carried_on(partial_ref, carried_ref, growth_ref), w_ref) if side else outer_ref[...]
        for f in range(frames):
            ready[side, f] = residual(x_ref[f, place(row, strip)], mixed[f])
            send(ready.at[side, f], out_ref.at[f, place(row, strip)])
    for copy in copies:
        copy.wait()


def call(kernel, out_shape, in_specs, out_specs, scratch, flops, aliases=None, moved=1 << 20):
    return pl.pallas_call(
        kernel,
        out_shape=out_shape,
        in_specs=in_specs,
        out_specs=out_specs,
        scratch_shapes=scratch,
        input_output_aliases=aliases or {},
        compiler_params=pltpu.CompilerParams(vmem_limit_bytes=LIMIT),
        cost_estimate=pl.CostEstimate(flops=flops, bytes_accessed=moved, transcendentals=0),
    )


def swapped(value, axis, distance):
    return lax.ppermute(value, axis, [(i, i ^ distance) for i in range(lax.axis_size(axis))])


def swapped_between(value, lower):
    places, count = lax.axis_size("tm"), lax.axis_size("rows")
    pairs = []
    for place_in in range(places):
        for i in range(count):
            if place_in in (lower, lower + 1):
                pairs.append((place_in * count + i, (2 * lower + 1 - place_in) * count + i))
            else:
                pairs.append((place_in * count + i, place_in * count + (i ^ 1)))
    return lax.ppermute(value, ("tm", "rows"), pairs)


def across_chips(value):
    groups, count = lax.axis_size("groups"), lax.axis_size("rows")
    pairs = []
    for group in range(groups):
        for i in range(count):
            other = (i + 1 if i % 2 else i - 1) % count
            side = group
            if groups % 2 == 0 and i in (0, count - 1):
                other, side = i, group ^ 1
            pairs.append((group * count + i, side * count + other))
    return lax.ppermute(value, ("groups", "rows"), pairs)


def butterfly(value, decay, axis):
    count, mine = lax.axis_size(axis), lax.axis_index(axis)
    total, carried, distance = value, None, 1
    before = jnp.ones_like(decay)
    while distance < count:
        other = swapped(total, axis, distance).astype(F32)
        after = (mine & distance) != 0
        own = total.astype(F32)
        here = jnp.where(after, before * other, 0.0)
        carried = here if carried is None else carried + here
        if 2 * distance < count:
            earlier, later = jnp.where(after, other, own), jnp.where(after, own, other)
            total = (decay * earlier + later).astype(value.dtype)
            before = jnp.where(after, decay * before, before)
            decay = decay * decay
        distance *= 2
    return carried


def local(latents, weight_in, weight_out, decay_table, decay_index):
    frames, strip, width, channels = latents.shape
    shaped = jax.ShapeDtypeStruct
    row, last = (frames, width, channels), (width, channels)
    inside = (strip - 2, width, channels)
    row_f32, row_bf16, last_bf16 = shaped(row, F32), shaped(row, BF16), shaped(last, BF16)
    inside_bf16, middle_f32 = shaped(inside, BF16), shaped((frames,) + inside, F32)
    order = shaped((frames, 1, channels), F32)
    conv_flops = 2 * 9 * frames * strip * width * channels * channels
    taps = pltpu.VMEM((3, frames, strip, width, channels), F32)

    x_outer, x_second, x_inner = call(rows_kernel, (row_bf16,) * 3, [VMEM], (VMEM,) * 3, [], 2 * conv_flops)(latents)
    halo_outer = across_chips(x_outer)
    halo_inner = swapped(x_inner, "rows", 1)
    outer, middle, inner, sent, growth = call(
        drive_kernel,
        (row_f32, middle_f32, row_f32, inside_bf16, order),
        [VMEM] * 4,
        (VMEM,) * 5,
        [taps, pltpu.VMEM((strip, width, channels), F32)],
        SMALL,
    )(latents, weight_in, decay_table[None, :], decay_index[None, :])

    def edge(beyond, halo, mixed, growth, *more):
        kernel = functools.partial(drive_edge_kernel, beyond)
        out_shape = (row_f32, last_bf16, order) + more
        return call(kernel, out_shape, [VMEM] * 4, (VMEM,) * len(out_shape), [], SMALL)(halo, weight_in, growth, mixed)

    def arrived(halo, growth):
        return call(arrived_kernel, order, [VMEM] * 2, VMEM, [], SMALL, moved=SMALL)(halo, growth)

    def beyond_states(growth, halo_second):
        return call(beyond_states_kernel, (row_f32, order), [VMEM] * 5, (VMEM,) * 2, [], SMALL, moved=SMALL)(
            halo_second, halo_outer, x_outer, weight_in, growth
        )

    if lax.axis_size("tm") == 4:
        first = swapped_between(sent, 0)
        outer, sent_outer, growth = edge(from_outside, halo_outer, outer, growth)
        inner, sent_inner, growth, rounded = edge(from_inside, halo_inner, inner, growth, row_bf16)
        far_outer = swapped(sent_outer, "tm", 2)
        x_second = call(later_kernel, row_bf16, [VMEM] * 2, VMEM, [], SMALL, moved=SMALL)(x_second, growth)
        halo_second = across_chips(x_second)
        inner_partial = swapped(rounded, "rows", 1)
        near_inner = swapped(sent_inner, "tm", 1)
        total, growth = call(relay_kernel, (inside_bf16, order), [VMEM] * 3, (VMEM,) * 2, [], SMALL)(sent, first, growth)
        second = swapped_between(total, 1)
        relayed_outer, growth = call(far_relay_kernel, (last_bf16, order), [VMEM] * 3, (VMEM,) * 2, [], LONG)(sent_outer, far_outer, growth)
        near_outer = swapped(relayed_outer, "tm", 1)
        total_inner, growth = call(pair_kernel, (last_bf16, order), [VMEM] * 3, (VMEM,) * 2, [], LONG)(sent_inner, near_inner, growth)
        far_inner = swapped(total_inner, "tm", 2)
        growth = arrived(halo_second, growth)
        message, growth = call(relay_kernel, (inside_bf16, order), [VMEM] * 3, (VMEM,) * 2, [], SMALL)(sent, second, growth)
        third = swapped_between(message, 2)
        states_outer, growth, carried_outer = call(
            far_states_kernel, (row_bf16, order, last_bf16), [VMEM] * 4, (VMEM,) * 3, [], LONG
        )(outer, far_outer, near_outer, growth)
        halo_carried = across_chips(carried_outer)
        halo_partial, growth = beyond_states(growth, halo_second)
        states_inner, growth, carried_inner = call(
            edge_states_kernel, (row_bf16, order, last_bf16), [VMEM] * 4, (VMEM,) * 3, [], SMALL
        )(inner, near_inner, far_inner, growth)
        inner_carried = swapped(carried_inner, "rows", 1)
    else:
        inner, sent_inner, growth, rounded = edge(from_inside, halo_inner, inner, growth, row_bf16)
        outer, sent_outer, growth = edge(from_outside, halo_outer, outer, growth)
        over = growth[frames - 1]
        halo_partial, growth = beyond_states(growth, across_chips(x_second))
        inner_partial = swapped(rounded, "rows", 1)
        carried_outer, carried_inner = butterfly(sent_outer, over, "tm"), butterfly(sent_inner, over, "tm")
        states_outer = (outer + growth * carried_outer[None]).astype(BF16)
        states_inner = (inner + growth * carried_inner[None]).astype(BF16)
        first = second = third = butterfly(sent, over, "tm").astype(BF16)
        halo_carried = across_chips(carried_outer.astype(BF16))
        inner_carried = swapped(carried_inner.astype(BF16), "rows", 1)
    ends = call(mix_ends_kernel, (row_f32, middle_f32, row_f32), [VMEM] * 3, (VMEM,) * 3, [], SMALL)(
        states_outer, states_inner, weight_out
    )
    outer, middle, inner = call(
        mix_inside_kernel,
        (row_f32, shaped((frames,) + inside, BF16), row_f32),
        [VMEM] * 10,
        (VMEM,) * 3,
        [taps, pltpu.VMEM((strip, width, channels), F32)],
        SMALL,
    )(first, second, third, growth, middle, weight_out, *ends, latents)
    outer = call(mix_beyond_kernel, row_f32, [VMEM] * 5, VMEM, [], SMALL)(
        halo_partial, halo_carried, growth, weight_out, outer
    )
    return call(
        finish_kernel,
        shaped(latents.shape, BF16),
        [VMEM] * 8,
        ANY,
        [pltpu.VMEM((2,) + row, BF16), pltpu.SemaphoreType.DMA((3 * frames,))],
        SMALL,
    )(inner_partial, inner_carried, growth, weight_out, outer, inner, middle, latents)


def solution(mesh):
    in_specs = (P(("groups", "tm"), "rows", None, None), P(), P(), P(), P())
    out_specs = P(("groups", "tm"), "rows", None, None)
    return jax.shard_map(local, mesh=mesh, in_specs=in_specs, out_specs=out_specs, check_vma=False)
```

```python
import functools

import jax
import jax.numpy as jnp
from jax import lax
from jax.experimental import pallas as pl
from jax.experimental.pallas import tpu as pltpu
from jax.sharding import PartitionSpec as P

VMEM = pl.BlockSpec(memory_space=pltpu.VMEM)
ANY = pl.BlockSpec(memory_space=pl.ANY)
SMALL = 1000
LONG = 3000000000
LIMIT = 24 * 1024 * 1024
F32, BF16 = jnp.float32, jnp.bfloat16


def turned():
    return lax.axis_index("rows") % 2


def place(row, count):
    return jnp.where(turned() == 1, count - 1 - row, row)


def matmul(rows, weight):
    lead, depth = rows.shape[:-1], rows.shape[-1]
    flat = jnp.dot(rows.reshape(-1, depth), weight, preferred_element_type=F32)
    return flat.reshape(*lead, weight.shape[-1])


def join_columns(left, middle, right):
    width = middle.shape[-2]
    axis = middle.ndim - 2
    column = lax.broadcasted_iota(jnp.int32, middle.shape, axis)
    left = jnp.where(column == 0, 0.0, pltpu.roll(left, 1, axis))
    right = jnp.where(column == width - 1, 0.0, pltpu.roll(right, width - 1, axis))
    return left + middle + right


def own_rows(x_ref, w_ref, taps):
    frames, strip = x_ref.shape[:2]
    for q in range(3):
        for f in range(frames):
            taps[q, f] = matmul(x_ref[f], w_ref[1, q])
            taps[q, f, 1:] += matmul(x_ref[f, : strip - 1], w_ref[0, q])
            taps[q, f, : strip - 1] += matmul(x_ref[f, 1:], w_ref[2, q])


def from_outside(halo_ref, w_ref):
    mine, count = lax.axis_index("rows"), lax.axis_size("rows")
    halo = halo_ref[...]
    inside = jnp.logical_and(mine > 0, mine < count - 1)
    halo = jnp.where(inside, halo, jnp.zeros_like(halo))
    return join_columns(*[matmul(halo, w_ref[place(0, 3), q]) for q in range(3)])


def from_inside(halo_ref, w_ref):
    return join_columns(*[matmul(halo_ref[...], w_ref[place(2, 3), q]) for q in range(3)])


def rows_kernel(x_ref, outer_ref, second_ref, inner_ref):
    frames, strip = x_ref.shape[:2]
    for f in range(frames):
        second_ref[f] = x_ref[f, place(1, strip)]
        outer_ref[f] = x_ref[f, place(0, strip)]
        inner_ref[f] = x_ref[f, place(strip - 1, strip)]


def drive_kernel(x_ref, w_ref, table_ref, index_ref, outer_ref, middle_ref, inner_ref, sent_ref, growth_ref, taps, states):
    frames, strip = x_ref.shape[:2]
    own_rows(x_ref, w_ref, taps)
    index = index_ref[...]
    decay = jnp.zeros(index.shape, F32)
    for level in range(table_ref.shape[1]):
        decay = jnp.where(index == level, table_ref[:, level : level + 1], decay)
    growth = decay
    state = None
    for f in range(frames):
        growth_ref[f] = growth
        growth = growth * decay
        driven = join_columns(taps[0, f], taps[1, f], taps[2, f])
        state = driven if state is None else decay.reshape(1, 1, -1) * state + driven
        states[...] = state
        outer_ref[f] = states[place(0, strip)]
        middle_ref[f] = state[1 : strip - 1]
        inner_ref[f] = states[place(strip - 1, strip)]
    sent_ref[...] = state[1 : strip - 1].astype(BF16)


def drive_edge_kernel(beyond, halo_ref, w_ref, growth_ref, row_ref, result_ref, sent_ref, order_ref, *rounded_ref):
    frames = row_ref.shape[0]
    driven = beyond(halo_ref, w_ref)
    decay = growth_ref[0]
    more = None
    for f in range(frames):
        more = driven[f] if more is None else decay * more + driven[f]
        state = row_ref[f] + more
        result_ref[f] = state
        for ref in rounded_ref:
            ref[f] = state.astype(BF16)
    sent_ref[...] = state.astype(BF16)
    order_ref[...] = growth_ref[...]


def later_kernel(x_ref, growth_ref, out_ref):
    out_ref[...] = x_ref[...]


def arrived_kernel(halo_ref, growth_ref, order_ref):
    order_ref[...] = growth_ref[...]


def beyond_states_kernel(second_ref, halo_ref, outer_ref, w_ref, growth_ref, result_ref, order_ref):
    above, level, below = second_ref[...], halo_ref[...], outer_ref[...]
    driven = join_columns(
        *[
            matmul(above, w_ref[place(0, 3), q]) + matmul(level, w_ref[1, q]) + matmul(below, w_ref[place(2, 3), q])
            for q in range(3)
        ]
    )
    state = None
    for f in range(driven.shape[0]):
        state = driven[f] if state is None else growth_ref[0] * state + driven[f]
        result_ref[f] = state
    order_ref[...] = growth_ref[...]


def pair_kernel(own_ref, other_ref, growth_ref, total_ref, order_ref):
    over = growth_ref[growth_ref.shape[0] - 1]
    own, other = own_ref[...].astype(F32), other_ref[...].astype(F32)
    after = lax.axis_index("tm") % 2 == 1
    earlier, later = jnp.where(after, other, own), jnp.where(after, own, other)
    total_ref[...] = (over * earlier + later).astype(BF16)
    order_ref[...] = growth_ref[...]


def edge_states_kernel(row_ref, near_ref, far_ref, growth_ref, states_ref, order_ref, carried_ref):
    frames = row_ref.shape[0]
    over = growth_ref[frames - 1]
    mine = lax.axis_index("tm")
    near, far = near_ref[...].astype(F32), far_ref[...].astype(F32)
    far = jnp.where(mine >= 2, far, 0.0)
    carried = jnp.where(mine % 2 == 1, over * far + near, far)
    carried_ref[...] = carried.astype(BF16)
    for f in range(frames):
        states_ref[f] = (row_ref[f] + growth_ref[f] * carried).astype(BF16)
    order_ref[...] = growth_ref[...]


def by_hop(first_ref, second_ref, third_ref):
    mine = lax.axis_index("tm")
    carried = third_ref[...].astype(F32)
    for hop, ref in enumerate((first_ref, second_ref)):
        carried = jnp.where(mine == hop + 1, ref[...].astype(F32), carried)
    return jnp.where(mine == 0, 0.0, carried)


def far_relay_kernel(own_ref, far_ref, growth_ref, message_ref, order_ref):
    over = growth_ref[growth_ref.shape[0] - 1]
    mine = lax.axis_index("tm")
    far = jnp.where(mine >= 2, far_ref[...].astype(F32), 0.0)
    message = jnp.where(mine % 2 == 1, far, over * over * far + own_ref[...].astype(F32))
    message_ref[...] = message.astype(BF16)
    order_ref[...] = growth_ref[...]


def far_states_kernel(row_ref, far_ref, near_ref, growth_ref, states_ref, order_ref, carried_ref):
    frames = row_ref.shape[0]
    mine = lax.axis_index("tm")
    far = jnp.where(mine >= 2, far_ref[...].astype(F32), 0.0)
    near = jnp.where(mine >= 1, near_ref[...].astype(F32), 0.0)
    carried = near + growth_ref[frames - 1] * far
    carried_ref[...] = carried.astype(BF16)
    for f in range(frames):
        states_ref[f] = (row_ref[f] + growth_ref[f] * carried).astype(BF16)
    order_ref[...] = growth_ref[...]


def relay_kernel(own_ref, before_ref, growth_ref, message_ref, order_ref):
    over = growth_ref[growth_ref.shape[0] - 1]
    message_ref[...] = (over * before_ref[...].astype(F32) + own_ref[...].astype(F32)).astype(BF16)
    order_ref[...] = growth_ref[...]


def residual(x, mixed):
    return (x.astype(F32) + jax.nn.gelu(mixed)).astype(BF16)


def mix_ends_kernel(outer_in, inner_in, w_ref, outer_ref, middle_ref, inner_ref):
    frames, inside = middle_ref.shape[:2]
    outer, inner = outer_in[...], inner_in[...]
    first = jnp.where(turned() == 1, inner, outer)
    last = jnp.where(turned() == 1, outer, inner)
    parts = [[[] for _ in range(inside)] for _ in range(3)]
    ends = []
    for q in range(3):
        ends.append(matmul(jnp.concatenate([outer, inner]), w_ref[1, q]))
        parts[q][0].append(matmul(first, w_ref[0, q]))
        parts[q][inside - 1].append(matmul(last, w_ref[2, q]))
    for row in range(inside):
        if parts[0][row]:
            middle_ref[:, row] = join_columns(*[sum(parts[q][row]) for q in range(3)])
        else:
            middle_ref[:, row] = jnp.zeros(first.shape, F32)
    ends = join_columns(*ends)
    outer_ref[...] = ends[:frames]
    inner_ref[...] = ends[frames:]


def mix_inside_kernel(
    first_ref, second_ref, third_ref, growth_ref, states_ref, w_ref, outer_in, middle_in, inner_in, x_ref,
    outer_ref, middle_ref, inner_ref, taps, mixed,
):
    frames, strip = x_ref.shape[:2]
    mine = lax.axis_index("tm")
    carried = third_ref[...].astype(F32)
    for hop, ref in enumerate((first_ref, second_ref)):
        carried = jnp.where(mine == hop + 1, ref[...].astype(F32), carried)
    carried = jnp.where(mine == 0, 0.0, carried)
    states = (states_ref[...] + growth_ref[...][:, None] * carried[None]).astype(BF16)
    for q in range(3):
        above, level, below = (matmul(states, w_ref[tap, q]) for tap in (2, 1, 0))
        for f in range(frames):
            taps[q, f, 1 : strip - 1] = level[f]
            taps[q, f, 0] = above[f, 0]
            taps[q, f, strip - 1] = below[f, strip - 3]
            if strip > 3:
                taps[q, f, 1 : strip - 2] += above[f, 1:]
                taps[q, f, 2 : strip - 1] += below[f, : strip - 3]
    for f in range(frames):
        mixed[...] = join_columns(taps[0, f], taps[1, f], taps[2, f])
        outer_ref[f] = outer_in[f] + mixed[place(0, strip)]
        inner_ref[f] = inner_in[f] + mixed[place(strip - 1, strip)]
        middle_ref[f] = residual(x_ref[f, 1 : strip - 1], middle_in[f] + mixed[1 : strip - 1])


def carried_on(partial_ref, carried_ref, growth_ref):
    return (partial_ref[...].astype(F32) + growth_ref[...] * carried_ref[...].astype(F32)[None]).astype(BF16)


def mix_beyond_kernel(partial_ref, carried_ref, growth_ref, w_ref, outer_in, outer_ref):
    outer_ref[...] = outer_in[...] + from_outside(carried_on(partial_ref, carried_ref, growth_ref), w_ref)


def finish_kernel(partial_ref, carried_ref, growth_ref, w_ref, outer_ref, inner_ref, middle_ref, x_ref, out_ref, ready, sems):
    frames, strip = x_ref.shape[:2]
    copies = []

    def send(source, target):
        copies.append(pltpu.make_async_copy(source, target, sems.at[len(copies)]))
        copies[-1].start()

    for f in range(frames):
        send(middle_ref.at[f], out_ref.at[f, 1 : strip - 1])
    for side, row in ((0, 0), (1, strip - 1)):
        mixed = inner_ref[...] + from_inside(carried_on(partial_ref, carried_ref, growth_ref), w_ref) if side else outer_ref[...]
        for f in range(frames):
            ready[side, f] = residual(x_ref[f, place(row, strip)], mixed[f])
            send(ready.at[side, f], out_ref.at[f, place(row, strip)])
    for copy in copies:
        copy.wait()


def call(kernel, out_shape, in_specs, out_specs, scratch, flops, aliases=None, moved=1 << 20):
    return pl.pallas_call(
        kernel,
        out_shape=out_shape,
        in_specs=in_specs,
        out_specs=out_specs,
        scratch_shapes=scratch,
        input_output_aliases=aliases or {},
        compiler_params=pltpu.CompilerParams(vmem_limit_bytes=LIMIT),
        cost_estimate=pl.CostEstimate(flops=flops, bytes_accessed=moved, transcendentals=0),
    )


def swapped(value, axis, distance):
    return lax.ppermute(value, axis, [(i, i ^ distance) for i in range(lax.axis_size(axis))])


def swapped_between(value, lower):
    places, count = lax.axis_size("tm"), lax.axis_size("rows")
    pairs = []
    for place_in in range(places):
        for i in range(count):
            if place_in in (lower, lower + 1):
                pairs.append((place_in * count + i, (2 * lower + 1 - place_in) * count + i))
            else:
                pairs.append((place_in * count + i, place_in * count + (i ^ 1)))
    return lax.ppermute(value, ("tm", "rows"), pairs)


def across_chips(value):
    groups, count = lax.axis_size("groups"), lax.axis_size("rows")
    pairs = []
    for group in range(groups):
        for i in range(count):
            other = (i + 1 if i % 2 else i - 1) % count
            side = group
            if groups % 2 == 0 and i in (0, count - 1):
                other, side = i, group ^ 1
            pairs.append((group * count + i, side * count + other))
    return lax.ppermute(value, ("groups", "rows"), pairs)


def butterfly(value, decay, axis):
    count, mine = lax.axis_size(axis), lax.axis_index(axis)
    total, carried, distance = value, None, 1
    before = jnp.ones_like(decay)
    while distance < count:
        other = swapped(total, axis, distance).astype(F32)
        after = (mine & distance) != 0
        own = total.astype(F32)
        here = jnp.where(after, before * other, 0.0)
        carried = here if carried is None else carried + here
        if 2 * distance < count:
            earlier, later = jnp.where(after, other, own), jnp.where(after, own, other)
            total = (decay * earlier + later).astype(value.dtype)
            before = jnp.where(after, decay * before, before)
            decay = decay * decay
        distance *= 2
    return carried


def local(latents, weight_in, weight_out, decay_table, decay_index):
    frames, strip, width, channels = latents.shape
    shaped = jax.ShapeDtypeStruct
    row, last = (frames, width, channels), (width, channels)
    inside = (strip - 2, width, channels)
    row_f32, row_bf16, last_bf16 = shaped(row, F32), shaped(row, BF16), shaped(last, BF16)
    inside_bf16, middle_f32 = shaped(inside, BF16), shaped((frames,) + inside, F32)
    order = shaped((frames, 1, channels), F32)
    conv_flops = 2 * 9 * frames * strip * width * channels * channels
    taps = pltpu.VMEM((3, frames, strip, width, channels), F32)

    x_outer, x_second, x_inner = call(rows_kernel, (row_bf16,) * 3, [VMEM], (VMEM,) * 3, [], 2 * conv_flops)(latents)
    halo_outer = across_chips(x_outer)
    halo_inner = swapped(x_inner, "rows", 1)
    outer, middle, inner, sent, growth = call(
        drive_kernel,
        (row_f32, middle_f32, row_f32, inside_bf16, order),
        [VMEM] * 4,
        (VMEM,) * 5,
        [taps, pltpu.VMEM((strip, width, channels), F32)],
        SMALL,
    )(latents, weight_in, decay_table[None, :], decay_index[None, :])

    def edge(beyond, halo, mixed, growth, *more):
        kernel = functools.partial(drive_edge_kernel, beyond)
        out_shape = (row_f32, last_bf16, order) + more
        return call(kernel, out_shape, [VMEM] * 4, (VMEM,) * len(out_shape), [], SMALL)(halo, weight_in, growth, mixed)

    def arrived(halo, growth):
        return call(arrived_kernel, order, [VMEM] * 2, VMEM, [], SMALL, moved=SMALL)(halo, growth)

    def beyond_states(growth, halo_second):
        return call(beyond_states_kernel, (row_f32, order), [VMEM] * 5, (VMEM,) * 2, [], SMALL, moved=SMALL)(
            halo_second, halo_outer, x_outer, weight_in, growth
        )

    if lax.axis_size("tm") == 4:
        first = swapped_between(sent, 0)
        outer, sent_outer, growth = edge(from_outside, halo_outer, outer, growth)
        inner, sent_inner, growth, rounded = edge(from_inside, halo_inner, inner, growth, row_bf16)
        far_outer = swapped(sent_outer, "tm", 2)
        x_second = call(later_kernel, row_bf16, [VMEM] * 2, VMEM, [], SMALL, moved=SMALL)(x_second, growth)
        halo_second = across_chips(x_second)
        inner_partial = swapped(rounded, "rows", 1)
        near_inner = swapped(sent_inner, "tm", 1)
        total, growth = call(relay_kernel, (inside_bf16, order), [VMEM] * 3, (VMEM,) * 2, [], SMALL)(sent, first, growth)
        second = swapped_between(total, 1)
        relayed_outer, growth = call(far_relay_kernel, (last_bf16, order), [VMEM] * 3, (VMEM,) * 2, [], LONG)(sent_outer, far_outer, growth)
        near_outer = swapped(relayed_outer, "tm", 1)
        total_inner, growth = call(pair_kernel, (last_bf16, order), [VMEM] * 3, (VMEM,) * 2, [], LONG)(sent_inner, near_inner, growth)
        far_inner = swapped(total_inner, "tm", 2)
        growth = arrived(halo_second, growth)
        message, growth = call(relay_kernel, (inside_bf16, order), [VMEM] * 3, (VMEM,) * 2, [], SMALL)(sent, second, growth)
        third = swapped_between(message, 2)
        states_outer, growth, carried_outer = call(
            far_states_kernel, (row_bf16, order, last_bf16), [VMEM] * 4, (VMEM,) * 3, [], LONG
        )(outer, far_outer, near_outer, growth)
        halo_carried = across_chips(carried_outer)
        states_inner, growth, carried_inner = call(
            edge_states_kernel, (row_bf16, order, last_bf16), [VMEM] * 4, (VMEM,) * 3, [], SMALL
        )(inner, near_inner, far_inner, growth)
        inner_carried = swapped(carried_inner, "rows", 1)
        halo_partial, growth = beyond_states(growth, halo_second)
    else:
        inner, sent_inner, growth, rounded = edge(from_inside, halo_inner, inner, growth, row_bf16)
        outer, sent_outer, growth = edge(from_outside, halo_outer, outer, growth)
        over = growth[frames - 1]
        halo_partial, growth = beyond_states(growth, across_chips(x_second))
        inner_partial = swapped(rounded, "rows", 1)
        carried_outer, carried_inner = butterfly(sent_outer, over, "tm"), butterfly(sent_inner, over, "tm")
        states_outer = (outer + growth * carried_outer[None]).astype(BF16)
        states_inner = (inner + growth * carried_inner[None]).astype(BF16)
        first = second = third = butterfly(sent, over, "tm").astype(BF16)
        halo_carried = across_chips(carried_outer.astype(BF16))
        inner_carried = swapped(carried_inner.astype(BF16), "rows", 1)
    ends = call(mix_ends_kernel, (row_f32, middle_f32, row_f32), [VMEM] * 3, (VMEM,) * 3, [], SMALL)(
        states_outer, states_inner, weight_out
    )
    outer, middle, inner = call(
        mix_inside_kernel,
        (row_f32, shaped((frames,) + inside, BF16), row_f32),
        [VMEM] * 10,
        (VMEM,) * 3,
        [taps, pltpu.VMEM((strip, width, channels), F32)],
        SMALL,
    )(first, second, third, growth, middle, weight_out, *ends, latents)
    outer = call(mix_beyond_kernel, row_f32, [VMEM] * 5, VMEM, [], SMALL)(
        halo_partial, halo_carried, growth, weight_out, outer
    )
    return call(
        finish_kernel,
        shaped(latents.shape, BF16),
        [VMEM] * 8,
        ANY,
        [pltpu.VMEM((2,) + row, BF16), pltpu.SemaphoreType.DMA((3 * frames,))],
        SMALL,
    )(inner_partial, inner_carried, growth, weight_out, outer, inner, middle, latents)


def solution(mesh):
    in_specs = (P(("groups", "tm"), "rows", None, None), P(), P(), P(), P())
    out_specs = P(("groups", "tm"), "rows", None, None)
    return jax.shard_map(local, mesh=mesh, in_specs=in_specs, out_specs=out_specs, check_vma=False)
```
